32 devices in a mesh: group: 2 (over x), dp: 16 (over z, y, core).
Axes of the slice: x: 2, y: 2, z: 4, core: 2. Of those that a mesh axis runs over, the one named last changes fastest.
Arguments:
- candidate_queries: bfloat16 [256, 8, 16, 4096], P(('group', 'dp')), parts along dimension 0, may hold values from -10 to 10
- target_states: bfloat16 [256, 32, 1024], P(('group', 'dp')), parts along dimension 0, may hold values from -4 to 4
- target_queries: bfloat16 [256, 32, 4096], P(('group', 'dp')), parts along dimension 0, may hold values from -10 to 10
- candidate_states: bfloat16 [2048, 16, 1024], P(('group', 'dp')), parts along dimension 0, may hold values from -4 to 4
- target_length: int32 [256], P(('group', 'dp')), parts along dimension 0, may hold values from 2 to 32
- candidate_length: int32 [256, 8], P(('group', 'dp')), parts along dimension 0, may hold values from 2 to 16
- candidate_row: int32 [256, 8], P(('group', 'dp')), parts along dimension 0, may hold values from 0 to 63, as said below
- direct_readout: bfloat16 [4096], replicated, may hold values from -0.5 to 0.5
- channel_readout: bfloat16 [4096], replicated, may hold values from -0.5 to 0.5
Outputs:
- rescored: float32 [2048], P(('group', 'dp')), parts along dimension 0
The draws below stay inside these ranges and needn't reach their ends.
There are 2 independent parts, one for each index of `group`. The reference program is written for one: setup_inputs(seed, part) draws one part's arguments, and reference() takes and returns one part's arrays. A program takes and returns all parts, laid end to end along the dimension named above; an argument that names none is the same for every part. Nothing has to cross between parts.
Inputs may be any that keep to these rules, and one draw needn't show every extreme that they name: `candidate_row`: on the 8 targets of each aligned block (targets b * 8 to (b + 1) * 8 - 1), the 64 entries hold every value from 0 to 63 once.
All inputs are finite; a program needn't handle non-finite values.
Results may differ from the reference program's by a relative error of at most 0.0021.
Values may be sent and summed in bfloat16 or wider, within the bound.
No kernel may reach another device: no remote copies, remote signals or barrier semaphores. Data moves between devices by JAX's collectives and lax.ppermute only.
A program may use at most 128 MiB of HBM per device.

```python
import math
import jax
import jax.numpy as jnp
from jax import lax

TGT_DEV = 8
SLOTS = 8
TARGET_TOKENS = 32
SOURCE_TOKENS = 16
QUERY_HEADS = 32
KEY_VALUE_HEADS = 4
HEAD_SIZE = 128
QW = 4096
PART_TARGETS = 128
CAND_DEV = 64
CANDIDATE_PAIRS = 1024
PEER_ROWS = 4


def starting_values(key, shape):
    return jax.random.truncated_normal(jax.random.fold_in(key, 3), -4.0, 4.0, shape)


def draw_candidate_queries(key, part):
    value_rows = starting_values(jax.random.fold_in(key, 21), (PART_TARGETS, SLOTS, SOURCE_TOKENS, QUERY_HEADS * HEAD_SIZE))
    return value_rows.astype(jnp.bfloat16)


def draw_target_states(key, part):
    value_rows = starting_values(jax.random.fold_in(key, 22), (PART_TARGETS, TARGET_TOKENS, 2 * KEY_VALUE_HEADS * HEAD_SIZE))
    return value_rows.astype(jnp.bfloat16)


def draw_target_queries(key, part):
    value_rows = starting_values(jax.random.fold_in(key, 23), (PART_TARGETS, TARGET_TOKENS, QUERY_HEADS * HEAD_SIZE))
    return value_rows.astype(jnp.bfloat16)


def draw_candidate_states(key, part):
    value_rows = starting_values(jax.random.fold_in(key, 24), (CANDIDATE_PAIRS, SOURCE_TOKENS, 2 * KEY_VALUE_HEADS * HEAD_SIZE))
    return value_rows.astype(jnp.bfloat16)


def draw_candidate_row(key, part):
    blocks = PART_TARGETS // TGT_DEV
    block_keys = jax.random.split(jax.random.fold_in(key, 31), blocks)
    orders = jax.vmap(lambda block_key: jax.random.permutation(block_key, CAND_DEV))(block_keys)
    return orders.reshape(PART_TARGETS, SLOTS).astype(jnp.int32)


def touch_ends(array, key, smallest, high):
    longest = array.shape.index(max(array.shape))
    spots = []
    for shift in (0, 1):
        where = [jax.random.randint(jax.random.fold_in(key, axis), (), 0, length) for axis, length in enumerate(array.shape)]
        where[longest] = (where[longest] + shift) % array.shape[longest]
        spots.append(tuple(where))
    return array.at[spots[0]].set(smallest).at[spots[1]].set(high)


def bell_draw(key, extent, scale, bound, held_as=jnp.bfloat16):
    return jnp.clip(scale * jax.random.normal(key, extent, jnp.float32), -bound, bound).astype(held_as)


def setup_inputs(seed: int = 0, part: int = 0) -> dict:
    keys = jax.random.split(jax.random.key(seed), 10)
    own_keys = jax.random.split(jax.random.fold_in(keys[9], part), 10)
    return {
        "candidate_queries": draw_candidate_queries(jax.random.fold_in(jax.random.fold_in(keys[9], part), 71), part),
        "target_states": draw_target_states(jax.random.fold_in(jax.random.fold_in(keys[9], part), 71), part),
        "target_queries": draw_target_queries(jax.random.fold_in(jax.random.fold_in(keys[9], part), 71), part),
        "candidate_states": draw_candidate_states(jax.random.fold_in(jax.random.fold_in(keys[9], part), 71), part),
        "target_length": touch_ends(jax.random.randint(own_keys[4], (PART_TARGETS,), 2, TARGET_TOKENS + 1), jax.random.fold_in(own_keys[4], 1), 2, TARGET_TOKENS).astype(jnp.int32),
        "candidate_length": touch_ends(jax.random.randint(own_keys[5], (PART_TARGETS, SLOTS), 2, SOURCE_TOKENS + 1), jax.random.fold_in(own_keys[5], 1), 2, SOURCE_TOKENS).astype(jnp.int32),
        "candidate_row": draw_candidate_row(jax.random.fold_in(jax.random.fold_in(keys[9], part), 71), part),
        "direct_readout": bell_draw(keys[7], (QW,), HEAD_SIZE ** -0.5, 0.5),
        "channel_readout": bell_draw(keys[8], (QW,), HEAD_SIZE ** -0.5, 0.5),
    }


masked_score = -1e+30

def attend_one(query_rows, hidden_states, length):
    count_of_rows = query_rows.shape[0]
    length_of_keys = hidden_states.shape[0]
    grouped_heads = query_rows.reshape(count_of_rows, KEY_VALUE_HEADS, QUERY_HEADS // KEY_VALUE_HEADS, HEAD_SIZE).astype(jnp.float32)
    split_halves = hidden_states.reshape(length_of_keys, 2, KEY_VALUE_HEADS, HEAD_SIZE).astype(jnp.float32)
    scores = jnp.einsum('rgqd,kgd->gqrk', grouped_heads, split_halves[:, 0]) * (1.0 / math.sqrt(HEAD_SIZE))
    usable = jnp.arange(length_of_keys, dtype=jnp.int32) < length
    scores = jnp.where(usable, scores, masked_score)
    highest = lax.optimization_barrier(jnp.max(scores, axis=-1, keepdims=True))
    weights = jnp.exp(scores - highest)
    rounded = lax.optimization_barrier((weights / lax.optimization_barrier(jnp.sum(weights, axis=-1, keepdims=True))).astype(jnp.bfloat16))
    mixture = jnp.einsum('gqrk,kgd->rgqd', rounded.astype(jnp.float32), split_halves[:, 1])
    return mixture.astype(jnp.bfloat16).reshape(count_of_rows, QUERY_HEADS * HEAD_SIZE)

def pooled(mixture, readout, length):
    tokens = jnp.dot(mixture, readout, preferred_element_type=jnp.float32)
    usable = jnp.arange(tokens.shape[0], dtype=jnp.int32) < length
    return jnp.sum(jnp.where(usable, tokens, 0.0)) / length.astype(jnp.float32)

def reference(candidate_queries, target_states, target_queries, candidate_states, target_length, candidate_length, candidate_row, direct_readout, channel_readout):
    target_index = jnp.arange(PART_TARGETS, dtype=jnp.int32)
    stored = candidate_row // PEER_ROWS * CAND_DEV + (target_index // TGT_DEV)[:, None] * PEER_ROWS + candidate_row % PEER_ROWS

    def score_target(index):
        lengths = candidate_length[index]
        own_length = target_length[index]

        def per_slot(slot):
            direct_mix = attend_one(candidate_queries[index, slot], target_states[index], own_length)
            direct = pooled(direct_mix, direct_readout, lengths[slot])
            hidden_states = candidate_states[stored[index, slot]]
            channel_mix = attend_one(target_queries[index], hidden_states, lengths[slot])
            channel = pooled(channel_mix, channel_readout, own_length)
            return direct + channel
        return jax.vmap(per_slot)(jnp.arange(SLOTS, dtype=jnp.int32))
    combined = lax.map(score_target, target_index)
    flat_rows = stored.reshape(CANDIDATE_PAIRS)
    return jnp.zeros((CANDIDATE_PAIRS,), jnp.float32).at[flat_rows].set(combined.reshape(CANDIDATE_PAIRS))
```

```python
import functools
import math

import jax
import jax.numpy as jnp
from jax import lax
from jax.experimental import pallas as pl
from jax.experimental.pallas import tpu as pltpu
from jax.sharding import PartitionSpec as P

KEY_VALUE_HEADS = 4
HEAD_SIZE = 128
LANES = 128
SUBLANES = 8
MASKED = -1e30

bf16 = jnp.bfloat16
f32 = jnp.float32


def dot_nt(a, b):
    return lax.dot_general(a, b, (((1,), (1,)), ((), ())), preferred_element_type=f32)


def dot_nn(a, b):
    return lax.dot_general(a, b, (((1,), (0,)), ((), ())), preferred_element_type=f32)


def iota(shape, axis):
    return lax.broadcasted_iota(jnp.int32, shape, axis)


def pack_kernel(rows, keys, states_ref, readout_ref, out_ref):
    peers = states_ref.shape[0]
    width = states_ref.shape[2] // 2
    heads = readout_ref.shape[0]
    share = heads // KEY_VALUE_HEADS
    copies = jnp.concatenate([readout_ref[...]] * (LANES // heads), axis=0)
    group = iota((LANES, HEAD_SIZE), 0) % heads // share
    spread = jnp.concatenate(
        [jnp.where(group == g, copies, jnp.zeros_like(copies)) for g in range(KEY_VALUE_HEADS)], axis=1
    )
    body = rows * keys
    lane = iota((SUBLANES, LANES), 1)
    for p in range(peers):
        out_ref[p, :body, :] = states_ref[p, :, :width]
        read = dot_nt(states_ref[p, :, width:], spread)
        for r in range(rows):
            first = read[r * keys : r * keys + SUBLANES, :]
            second = read[r * keys + SUBLANES : r * keys + 2 * SUBLANES, :]
            value = jnp.where(lane < 2 * heads, first, second)
            high = value.astype(bf16).astype(f32)
            parts = jnp.where(lane % (2 * heads) < heads, high, value - high)
            out_ref[p, body : body + SUBLANES, r * LANES : (r + 1) * LANES] = parts.astype(bf16)


def direct_kernel(target_length, queries_ref, states_ref, readout_ref, length_ref, out_ref):
    t = pl.program_id(0)
    keys = states_ref.shape[1]
    width = states_ref.shape[2] // 2
    tokens = queries_ref.shape[1]
    slots = length_ref.shape[1]
    heads = readout_ref.shape[0]
    share = heads // KEY_VALUE_HEADS
    scale = math.log2(math.e) / math.sqrt(HEAD_SIZE)
    usable = iota((keys, share * tokens), 0) < target_length[t]
    total = jnp.zeros((1, tokens), f32)
    for g in range(KEY_VALUE_HEADS):
        k = states_ref[0, :, g * HEAD_SIZE : (g + 1) * HEAD_SIZE]
        v = states_ref[0, :, width + g * HEAD_SIZE : width + (g + 1) * HEAD_SIZE]
        q = jnp.concatenate(
            [
                queries_ref[0, :, h * HEAD_SIZE : (h + 1) * HEAD_SIZE]
                for h in range(g * share, (g + 1) * share)
            ],
            axis=0,
        )
        scores = jnp.where(usable, dot_nt(k, q), MASKED)
        weights = jnp.exp2((scores - jnp.max(scores, axis=0, keepdims=True)) * scale)
        read = dot_nt(v, readout_ref[g * share : (g + 1) * share, :])
        read = jnp.concatenate(
            [jnp.broadcast_to(read[:, h : h + 1], (keys, tokens)) for h in range(share)], axis=1
        )
        ratio = jnp.sum(weights * read, axis=0, keepdims=True) / jnp.sum(
            weights, axis=0, keepdims=True
        )
        for h in range(share):
            total = total + ratio[:, h * tokens : (h + 1) * tokens]
    source = tokens // slots
    lane = iota((slots, tokens), 1)
    length = length_ref[0]
    wanted = (lane // source == iota((slots, tokens), 0)) & (lane % source < length)
    out_ref[0] = jnp.where(wanted, jnp.broadcast_to(total, (slots, tokens)), 0.0) / length.astype(f32)


def channel_kernel(
    rows,
    place,
    row_at,
    target_length,
    arrived_ref,
    queries_ref,
    direct_ref,
    length_ref,
    row_ref,
    order_ref,
    half_order_ref,
    expand_ref,
    out_ref,
    keys_ref,
    read_ref,
):
    targets, tokens, _ = queries_ref.shape
    slots = direct_ref.shape[1]
    peers, _, width = arrived_ref.shape
    keys = keys_ref.shape[0] // slots
    body = rows * keys
    share = queries_ref.shape[2] // HEAD_SIZE // KEY_VALUE_HEADS
    columns = share * tokens
    scale = math.log2(math.e) / math.sqrt(HEAD_SIZE)
    lane = iota((slots, LANES), 1)
    gathered = jnp.zeros((slots, LANES), f32)
    position = iota((keys, slots, columns), 0)
    for t in range(targets):
        for s in range(slots):
            row = row_at[t, s]
            peer = row // rows
            r = row % rows
            keys_ref[s * keys : (s + 1) * keys, :] = arrived_ref[
                peer, pl.ds(pl.multiple_of(r * keys, keys), keys), :
            ]
            read_ref[s * SUBLANES : (s + 1) * SUBLANES, :] = arrived_ref[
                peer, body : body + SUBLANES, pl.ds(pl.multiple_of(r * LANES, LANES), LANES)
            ].astype(f32)
        key = dot_nn(order_ref[...], keys_ref[...]).astype(bf16)
        read = dot_nn(half_order_ref[...], read_ref[...].astype(bf16)).astype(bf16)
        read = dot_nn(read, expand_ref[...])
        length = jnp.concatenate([length_ref[t]] * (columns // LANES), axis=1)
        usable = position < length[None]
        total = jnp.zeros((slots, columns), f32)
        for g in range(KEY_VALUE_HEADS):
            q = jnp.concatenate(
                [
                    queries_ref[t, :, h * HEAD_SIZE : (h + 1) * HEAD_SIZE]
                    for h in range(g * share, (g + 1) * share)
                ],
                axis=0,
            )
            scores = dot_nt(key[:, g * HEAD_SIZE : (g + 1) * HEAD_SIZE], q)
            scores = jnp.where(usable, scores.reshape(keys, slots, columns), MASKED)
            weights = jnp.exp2((scores - jnp.max(scores, axis=0, keepdims=True)) * scale)
            half = KEY_VALUE_HEADS * columns
            value = jnp.concatenate(
                [
                    read[:, i * half + g * columns : i * half + (g + 1) * columns]
                    for i in range(keys // SUBLANES)
                ],
                axis=0,
            ).reshape(keys, slots, columns)
            total = total + jnp.sum(weights * value, axis=0) / jnp.sum(weights, axis=0)
        count = target_length[t]
        token = iota((slots, columns), 1) % tokens
        total = jnp.where(token < count, total, 0.0) / count.astype(f32)
        combined = direct_ref[t]
        for i in range(columns // LANES):
            combined = combined + total[:, i * LANES : (i + 1) * LANES]
        combined = jnp.sum(combined, axis=1, keepdims=True)
        gathered = gathered + jnp.where(row_ref[t] == lane, combined, 0.0)
    gathered = jnp.sum(gathered, axis=0, keepdims=True)
    at = iota((peers, LANES), 1)
    mine = iota((peers, LANES), 0) * rows
    out = jnp.zeros((peers, LANES), f32)
    for r in range(rows):
        sent = jnp.sum(jnp.where(at == mine + r, gathered, 0.0), axis=1, keepdims=True)
        out = out + jnp.where(at == place[0] * rows + r, sent, 0.0)
    out_ref[...] = out


def on_device(
    candidate_queries,
    target_states,
    target_queries,
    candidate_states,
    target_length,
    candidate_length,
    candidate_row,
    direct_readout,
    channel_readout,
    *,
    peers,
):
    targets, slots, keys, query_width = candidate_queries.shape
    tokens = target_queries.shape[1]
    candidates = candidate_states.shape[0]
    width = candidate_states.shape[2] // 2
    heads = query_width // HEAD_SIZE
    share = heads // KEY_VALUE_HEADS
    rows = candidates // peers
    columns = share * tokens
    assert keys == 2 * SUBLANES and slots == SUBLANES
    assert 4 * heads == LANES and slots * keys == LANES
    assert rows * LANES <= width and candidates <= LANES

    body = rows * keys
    chunk = body + SUBLANES
    step = max(1, peers // 4)
    packed = pl.pallas_call(
        functools.partial(pack_kernel, rows, keys),
        out_shape=jax.ShapeDtypeStruct((peers, chunk, width), bf16),
        grid=(peers // step,),
        in_specs=[
            pl.BlockSpec((step, body, 2 * width), lambda i: (i, 0, 0)),
            pl.BlockSpec((heads, HEAD_SIZE), lambda i: (0, 0)),
        ],
        out_specs=pl.BlockSpec((step, chunk, width), lambda i: (i, 0, 0)),
        compiler_params=pltpu.CompilerParams(vmem_limit_bytes=16 * 2**20),
        name="pack",
    )(
        candidate_states.reshape(peers, body, 2 * width),
        channel_readout.reshape(heads, HEAD_SIZE),
    )
    arrived = lax.all_to_all(packed, "dp", split_axis=0, concat_axis=0, tiled=True)

    length_lanes = jnp.broadcast_to(candidate_length[:, :, None], (targets, slots, LANES))
    row_lanes = jnp.broadcast_to(candidate_row[:, :, None], (targets, slots, LANES))
    direct = pl.pallas_call(
        direct_kernel,
        out_shape=jax.ShapeDtypeStruct((targets, slots, slots * keys), f32),
        grid_spec=pltpu.PrefetchScalarGridSpec(
            num_scalar_prefetch=1,
            grid=(targets,),
            in_specs=[
                pl.BlockSpec((1, slots * keys, query_width), lambda t, n: (t, 0, 0)),
                pl.BlockSpec((1, tokens, 2 * width), lambda t, n: (t, 0, 0)),
                pl.BlockSpec((heads, HEAD_SIZE), lambda t, n: (0, 0)),
                pl.BlockSpec((1, slots, LANES), lambda t, n: (t, 0, 0)),
            ],
            out_specs=pl.BlockSpec((1, slots, slots * keys), lambda t, n: (t, 0, 0)),
        ),
        compiler_params=pltpu.CompilerParams(vmem_limit_bytes=32 * 2**20),
        cost_estimate=pl.CostEstimate(
            flops=4 * candidate_queries.size * tokens,
            bytes_accessed=2 * candidate_queries.size,
            transcendentals=0,
        ),
        name="direct",
    )(
        target_length,
        candidate_queries.reshape(targets, slots * keys, query_width),
        target_states,
        direct_readout.reshape(heads, HEAD_SIZE),
        length_lanes,
    )

    pairs = slots * keys
    to = jnp.arange(pairs, dtype=jnp.int32)[:, None]
    come = jnp.arange(pairs, dtype=jnp.int32)[None, :]
    order = ((to % slots == come // keys) & (to // slots == come % keys)).astype(bf16)
    to, come = to[: pairs // 2], come[:, : pairs // 2]
    half_order = ((to % slots == come // SUBLANES) & (to // slots == come % SUBLANES)).astype(bf16)
    value = jnp.arange(LANES, dtype=jnp.int32)[:, None]
    column = jnp.arange(2 * heads * tokens, dtype=jnp.int32)[None, :]
    expand = (
        (value // (2 * heads) == column // (heads * tokens))
        & (value % heads == column // tokens % heads)
    ).astype(bf16)

    place = lax.axis_index("dp").astype(jnp.int32).reshape(1)
    vmem = pl.BlockSpec(memory_space=pltpu.VMEM)
    smem = pl.BlockSpec(memory_space=pltpu.SMEM)
    outgoing = pl.pallas_call(
        functools.partial(channel_kernel, rows),
        out_shape=jax.ShapeDtypeStruct((peers, LANES), f32),
        in_specs=[smem] * 3 + [vmem] * 8,
        out_specs=vmem,
        scratch_shapes=[
            pltpu.VMEM((slots * keys, width), bf16),
            pltpu.VMEM((slots * SUBLANES, LANES), f32),
        ],
        compiler_params=pltpu.CompilerParams(vmem_limit_bytes=32 * 2**20),
        name="channel",
    )(
        place,
        candidate_row,
        target_length,
        arrived,
        target_queries,
        direct,
        length_lanes,
        row_lanes,
        order,
        half_order,
        expand,
    )
    returned = lax.all_to_all(outgoing, "dp", split_axis=0, concat_axis=0, tiled=True)
    return jnp.sum(returned, axis=0)[:candidates]


def solution(mesh):
    in_specs = (
        P(("group", "dp"), None, None, None),
        P(("group", "dp"), None, None),
        P(("group", "dp"), None, None),
        P(("group", "dp"), None, None),
        P(("group", "dp")),
        P(("group", "dp"), None),
        P(("group", "dp"), None),
        P(),
        P(),
    )
    out_specs = P(("group", "dp"))
    return jax.shard_map(
        functools.partial(on_device, peers=mesh.shape["dp"]),
        mesh=mesh,
        in_specs=in_specs,
        out_specs=out_specs,
        check_vma=False,
    )
```

```python
import functools
import math

import jax
import jax.numpy as jnp
from jax import lax
from jax.experimental import pallas as pl
from jax.experimental.pallas import tpu as pltpu
from jax.sharding import PartitionSpec as P

KEY_VALUE_HEADS = 4
HEAD_SIZE = 128
LANES = 128
SUBLANES = 8
MASKED = -1e30
PACK_LIMIT = 60 * 2**20

bf16 = jnp.bfloat16
f32 = jnp.float32


def dot_nt(a, b):
    return lax.dot_general(a, b, (((1,), (1,)), ((), ())), preferred_element_type=f32)


def dot_nn(a, b):
    return lax.dot_general(a, b, (((1,), (0,)), ((), ())), preferred_element_type=f32)


def iota(shape, axis):
    return lax.broadcasted_iota(jnp.int32, shape, axis)


def pack_kernel(rows, keys, states_ref, readout_ref, out_ref, values_ref, read_ref, sent_ref, sems):
    peers, body, width = values_ref.shape
    half = width // 2
    heads = read_ref.shape[0]
    share = heads // KEY_VALUE_HEADS
    parts = (sems.shape[0] - 1) // 4
    step = peers // parts
    load_readout = pltpu.make_async_copy(readout_ref, read_ref, sems.at[0])
    load_readout.start()
    loads, moves, sends = [], [], []
    for i in range(parts):
        at = pl.ds(i * step, step)
        loads.append(
            pltpu.make_async_copy(
                states_ref.at[at, :, width:], values_ref.at[at], sems.at[1 + i]
            )
        )
        loads[i].start()
    for i in range(parts):
        at = pl.ds(i * step, step)
        for j in range(2):
            moves.append(
                pltpu.make_async_copy(
                    states_ref.at[at, :, j * half : (j + 1) * half],
                    sent_ref.at[at, j * body : (j + 1) * body, :],
                    sems.at[1 + (1 + j) * parts + i],
                )
            )
            moves[-1].start()
    load_readout.wait()
    repeated = jnp.concatenate([read_ref[...]] * (LANES // heads), axis=0)
    group = iota((LANES, HEAD_SIZE), 0) % heads // share
    spread = jnp.concatenate(
        [jnp.where(group == g, repeated, jnp.zeros_like(repeated)) for g in range(KEY_VALUE_HEADS)],
        axis=1,
    )
    lane = iota((keys, LANES), 1)
    for i in range(parts):
        loads[i].wait()
        read = dot_nt(values_ref[i * step : (i + 1) * step].reshape(step * body, width), spread)
        for p in range(step):
            for j in range(half // LANES):
                even = min(2 * j, rows - 1)
                odd = min(2 * j + 1, rows - 1)
                even = read[p * body + even * keys : p * body + (even + 1) * keys, :]
                odd = read[p * body + odd * keys : p * body + (odd + 1) * keys, :]
                value = jnp.where(lane < 2 * heads, even, odd)
                high = value.astype(bf16).astype(f32)
                value = jnp.where(lane % (2 * heads) < heads, high, value - high)
                sent_ref[i * step + p, 2 * body :, j * LANES : (j + 1) * LANES] = value.astype(bf16)
        moves[2 * i].wait()
        moves[2 * i + 1].wait()
        at = pl.ds(i * step, step)
        sends.append(
            pltpu.make_async_copy(sent_ref.at[at], out_ref.at[at], sems.at[1 + 3 * parts + i])
        )
        sends[i].start()
    for copy in sends:
        copy.wait()


def direct_kernel(target_length, queries_ref, states_ref, readout_ref, length_ref, out_ref):
    t = pl.program_id(0)
    keys = states_ref.shape[1]
    width = states_ref.shape[2] // 2
    tokens = queries_ref.shape[1]
    slots = length_ref.shape[1]
    heads = readout_ref.shape[0]
    share = heads // KEY_VALUE_HEADS
    scale = math.log2(math.e) / math.sqrt(HEAD_SIZE)
    usable = iota((keys, share * tokens), 0) < target_length[t]
    total = jnp.zeros((1, tokens), f32)
    for g in range(KEY_VALUE_HEADS):
        k = states_ref[0, :, g * HEAD_SIZE : (g + 1) * HEAD_SIZE]
        v = states_ref[0, :, width + g * HEAD_SIZE : width + (g + 1) * HEAD_SIZE]
        q = jnp.concatenate(
            [
                queries_ref[0, :, h * HEAD_SIZE : (h + 1) * HEAD_SIZE]
                for h in range(g * share, (g + 1) * share)
            ],
            axis=0,
        )
        scores = jnp.where(usable, dot_nt(k, q), MASKED)
        weights = jnp.exp2((scores - jnp.max(scores, axis=0, keepdims=True)) * scale)
        read = dot_nt(v, readout_ref[g * share : (g + 1) * share, :])
        read = jnp.concatenate(
            [jnp.broadcast_to(read[:, h : h + 1], (keys, tokens)) for h in range(share)], axis=1
        )
        ratio = jnp.sum(weights * read, axis=0, keepdims=True) / jnp.sum(
            weights, axis=0, keepdims=True
        )
        for h in range(share):
            total = total + ratio[:, h * tokens : (h + 1) * tokens]
    source = tokens // slots
    lane = iota((slots, tokens), 1)
    length = length_ref[0]
    wanted = (lane // source == iota((slots, tokens), 0)) & (lane % source < length)
    out_ref[0] = jnp.where(wanted, jnp.broadcast_to(total, (slots, tokens)), 0.0) / length.astype(f32)


def channel_kernel(
    rows,
    share,
    at_ref,
    arrived_ref,
    queries_ref,
    direct_ref,
    length_ref,
    row_ref,
    pick_ref,
    weight_ref,
    mine_ref,
    out_ref,
    keys_ref,
    read_ref,
):
    targets = queries_ref.shape[0]
    columns = queries_ref.shape[3]
    slots = direct_ref.shape[1]
    peers = out_ref.shape[0]
    keys = keys_ref.shape[2] // slots
    body = rows * keys
    heads = KEY_VALUE_HEADS * share
    per = arrived_ref.shape[1] // HEAD_SIZE
    scale = math.log2(math.e) / math.sqrt(HEAD_SIZE)
    lane = iota((slots, LANES), 1)
    position = iota((keys, slots, columns), 0)
    gathered = jnp.zeros((slots, LANES), f32)
    for t in range(targets):
        for s in range(slots):
            start = pl.multiple_of(at_ref[0, t * slots + s], keys)
            for j in range(KEY_VALUE_HEADS // per):
                key = arrived_ref[pl.ds(start + j * body, keys), :].astype(f32)
                for g in range(per):
                    keys_ref[t, j * per + g, pl.ds(s, keys, stride=slots), :] = key[
                        :, g * HEAD_SIZE : (g + 1) * HEAD_SIZE
                    ]
            start = pl.multiple_of(at_ref[1, t * slots + s], keys)
            across = pl.multiple_of(at_ref[2, t * slots + s], LANES)
            read_ref[t, pl.ds(s, keys, stride=slots), :] = arrived_ref[
                pl.ds(start, keys), pl.ds(across, LANES)
            ].astype(f32)
        read = read_ref[t]
        read = read + pltpu.roll(read, LANES - heads, 1)
        usable = position < jnp.concatenate([length_ref[t]] * (columns // LANES), axis=1)[None]
        total = jnp.zeros((slots, columns), f32)
        for g in range(KEY_VALUE_HEADS):
            scores = dot_nn(keys_ref[t, g].astype(bf16), queries_ref[t, g])
            scores = jnp.where(usable, scores.reshape(keys, slots, columns), MASKED)
            weights = jnp.exp2((scores - jnp.max(scores, axis=0, keepdims=True)) * scale)
            pick = pick_ref[t] + g * share
            value = jnp.concatenate(
                [
                    jnp.take_along_axis(read[i * slots : (i + 1) * slots, :], pick, axis=1)
                    for i in range(keys)
                ],
                axis=0,
            )
            value = jnp.concatenate([value] * (columns // LANES), axis=1)
            value = value.reshape(keys, slots, columns)
            total = total + jnp.sum(weights * value, axis=0) / jnp.sum(weights, axis=0)
        total = total * weight_ref[t : t + 1, :]
        combined = direct_ref[t]
        for i in range(columns // LANES):
            combined = combined + total[:, i * LANES : (i + 1) * LANES]
        combined = jnp.sum(combined, axis=1, keepdims=True)
        gathered = gathered + jnp.where(row_ref[t] == lane, combined, 0.0)
    gathered = jnp.sum(gathered, axis=0, keepdims=True)
    at = iota((peers, LANES), 1) - iota((peers, LANES), 0) * rows
    out = jnp.zeros((peers, LANES), f32)
    for r in range(rows):
        sent = jnp.sum(jnp.where(at == r, gathered, 0.0), axis=1, keepdims=True)
        out = out + jnp.where(mine_ref[...] == r, sent, 0.0)
    out_ref[...] = out


def on_device(
    candidate_queries,
    target_states,
    target_queries,
    candidate_states,
    target_length,
    candidate_length,
    candidate_row,
    direct_readout,
    channel_readout,
    *,
    peers,
):
    targets, slots, keys, query_width = candidate_queries.shape
    tokens = target_queries.shape[1]
    candidates = candidate_states.shape[0]
    width = candidate_states.shape[2] // 2
    heads = query_width // HEAD_SIZE
    share = heads // KEY_VALUE_HEADS
    rows = candidates // peers
    columns = share * tokens
    assert slots == SUBLANES and keys == 2 * SUBLANES and slots * keys == LANES
    assert 4 * heads == LANES and width == 4 * LANES and rows <= 4 and candidates <= LANES

    body = rows * keys
    chunk = 2 * body + keys
    parts = 4
    hbm = pl.BlockSpec(memory_space=pltpu.HBM)
    packed = pl.pallas_call(
        functools.partial(pack_kernel, rows, keys),
        out_shape=jax.ShapeDtypeStruct((peers, chunk, width // 2), bf16),
        in_specs=[hbm, hbm],
        out_specs=hbm,
        scratch_shapes=[
            pltpu.VMEM((peers, body, width), bf16),
            pltpu.VMEM((heads, HEAD_SIZE), bf16),
            pltpu.VMEM((peers, chunk, width // 2), bf16),
            pltpu.SemaphoreType.DMA((1 + 4 * parts,)),
        ],
        compiler_params=pltpu.CompilerParams(vmem_limit_bytes=PACK_LIMIT),
        name="pack",
    )(
        candidate_states.reshape(peers, body, 2 * width),
        channel_readout.reshape(heads, HEAD_SIZE),
    )
    arrived = lax.all_to_all(packed, "dp", split_axis=0, concat_axis=0, tiled=True)

    length_lanes = jnp.broadcast_to(candidate_length[:, :, None], (targets, slots, LANES))
    row_lanes = jnp.broadcast_to(candidate_row[:, :, None], (targets, slots, LANES))
    direct = pl.pallas_call(
        direct_kernel,
        out_shape=jax.ShapeDtypeStruct((targets, slots, slots * keys), f32),
        grid_spec=pltpu.PrefetchScalarGridSpec(
            num_scalar_prefetch=1,
            grid=(targets,),
            in_specs=[
                pl.BlockSpec((1, slots * keys, query_width), lambda t, n: (t, 0, 0)),
                pl.BlockSpec((1, tokens, 2 * width), lambda t, n: (t, 0, 0)),
                pl.BlockSpec((heads, HEAD_SIZE), lambda t, n: (0, 0)),
                pl.BlockSpec((1, slots, LANES), lambda t, n: (t, 0, 0)),
            ],
            out_specs=pl.BlockSpec((1, slots, slots * keys), lambda t, n: (t, 0, 0)),
        ),
        compiler_params=pltpu.CompilerParams(vmem_limit_bytes=32 * 2**20),
        cost_estimate=pl.CostEstimate(
            flops=4 * candidate_queries.size * tokens,
            bytes_accessed=2 * candidate_queries.size,
            transcendentals=0,
        ),
        name="direct",
    )(
        target_length,
        candidate_queries.reshape(targets, slots * keys, query_width),
        target_states,
        direct_readout.reshape(heads, HEAD_SIZE),
        length_lanes,
    )

    queries = target_queries.reshape(targets, tokens, KEY_VALUE_HEADS, share, HEAD_SIZE)
    queries = queries.transpose(0, 2, 4, 1, 3).reshape(
        targets, KEY_VALUE_HEADS, HEAD_SIZE, columns
    )
    flat = candidate_row.reshape(candidates)
    at = jnp.stack(
        [
            flat // rows * chunk + flat % rows * keys,
            flat // rows * chunk + 2 * body,
            flat % rows // 2 * LANES,
        ]
    )
    lanes = jnp.arange(LANES, dtype=jnp.int32)
    pick = lanes % share + row_lanes % rows % 2 * (2 * heads)
    token = jnp.arange(columns, dtype=jnp.int32)[None, :] // share
    count = target_length[:, None]
    weight = jnp.where(token < count, 1.0 / count.astype(f32), 0.0)
    mine = (lanes - lax.axis_index("dp").astype(jnp.int32) * rows)[None, :]
    vmem = pl.BlockSpec(memory_space=pltpu.VMEM)
    smem = pl.BlockSpec(memory_space=pltpu.SMEM)
    outgoing = pl.pallas_call(
        functools.partial(channel_kernel, rows, share),
        out_shape=jax.ShapeDtypeStruct((peers, LANES), f32),
        in_specs=[smem] + [vmem] * 8,
        out_specs=vmem,
        scratch_shapes=[
            pltpu.VMEM((targets, KEY_VALUE_HEADS, slots * keys, HEAD_SIZE), f32),
            pltpu.VMEM((targets, slots * keys, LANES), f32),
        ],
        compiler_params=pltpu.CompilerParams(vmem_limit_bytes=32 * 2**20),
        name="channel",
    )(
        at,
        arrived.reshape(peers * chunk, width // 2),
        queries,
        direct,
        length_lanes,
        row_lanes,
        pick,
        weight,
        mine,
    )
    returned = lax.all_to_all(outgoing, "dp", split_axis=0, concat_axis=0, tiled=True)
    return jnp.sum(returned, axis=0)[:candidates]


def solution(mesh):
    in_specs = (
        P(("group", "dp"), None, None, None),
        P(("group", "dp"), None, None),
        P(("group", "dp"), None, None),
        P(("group", "dp"), None, None),
        P(("group", "dp")),
        P(("group", "dp"), None),
        P(("group", "dp"), None),
        P(),
        P(),
    )
    out_specs = P(("group", "dp"))
    return jax.shard_map(
        functools.partial(on_device, peers=mesh.shape["dp"]),
        mesh=mesh,
        in_specs=in_specs,
        out_specs=out_specs,
        check_vma=False,
    )
```

```python
import functools
import math

import jax
import jax.numpy as jnp
from jax import lax
from jax.experimental import pallas as pl
from jax.experimental.pallas import tpu as pltpu
from jax.sharding import PartitionSpec as P

KEY_VALUE_HEADS = 4
HEAD_SIZE = 128
LANES = 128
SUBLANES = 8
MASKED = -1e30

bf16 = jnp.bfloat16
f32 = jnp.float32


def dot_nt(a, b):
    return lax.dot_general(a, b, (((1,), (1,)), ((), ())), preferred_element_type=f32)


def dot_nn(a, b):
    return lax.dot_general(a, b, (((1,), (0,)), ((), ())), preferred_element_type=f32)


def iota(shape, axis):
    return lax.broadcasted_iota(jnp.int32, shape, axis)


def pack_kernel(rows, keys, states_ref, readout_ref, out_ref, values_ref, read_ref, sent_ref, sems):
    peers, body, width = values_ref.shape
    half = width // 2
    heads = read_ref.shape[0]
    share = heads // KEY_VALUE_HEADS
    keep = [slice(0, body), slice(body, 2 * body), slice(2 * body, None)]
    loads = [
        pltpu.make_async_copy(
            states_ref.at[:, :, j * half : (j + 1) * half], sent_ref.at[:, keep[j], :], sems.at[j]
        )
        for j in range(2)
    ]
    loads.append(pltpu.make_async_copy(states_ref.at[:, :, width:], values_ref, sems.at[2]))
    loads.append(pltpu.make_async_copy(readout_ref, read_ref, sems.at[3]))
    sends = [
        pltpu.make_async_copy(sent_ref.at[:, keep[j], :], out_ref.at[:, keep[j], :], sems.at[4 + j])
        for j in range(3)
    ]
    for copy in loads:
        copy.start()
    for j in range(2):
        loads[j].wait()
        sends[j].start()
    loads[3].wait()
    repeated = jnp.concatenate([read_ref[...]] * (LANES // heads), axis=0)
    group = iota((LANES, HEAD_SIZE), 0) % heads // share
    spread = jnp.concatenate(
        [jnp.where(group == g, repeated, jnp.zeros_like(repeated)) for g in range(KEY_VALUE_HEADS)],
        axis=1,
    )
    lane = iota((keys, LANES), 1)
    loads[2].wait()
    read = dot_nt(values_ref[...].reshape(peers * body, width), spread)
    for p in range(peers):
        for j in range(half // LANES):
            even = min(2 * j, rows - 1)
            odd = min(2 * j + 1, rows - 1)
            even = read[p * body + even * keys : p * body + (even + 1) * keys, :]
            odd = read[p * body + odd * keys : p * body + (odd + 1) * keys, :]
            value = jnp.where(lane < 2 * heads, even, odd)
            high = value.astype(bf16).astype(f32)
            value = jnp.where(lane % (2 * heads) < heads, high, value - high)
            sent_ref[p, keep[2], j * LANES : (j + 1) * LANES] = value.astype(bf16)
    sends[2].start()
    for copy in sends:
        copy.wait()


def direct_kernel(
    target_length, at_ref, queries_ref, states_ref, readout_ref, length_ref, out_ref, place_ref
):
    t = pl.program_id(0)

    @pl.when(t == 0)
    def _():
        for i in range(at_ref.shape[0]):
            for j in range(at_ref.shape[1]):
                place_ref[i, j] = at_ref[i, j]

    keys = states_ref.shape[1]
    width = states_ref.shape[2] // 2
    tokens = queries_ref.shape[1]
    slots = length_ref.shape[1]
    heads = readout_ref.shape[0]
    share = heads // KEY_VALUE_HEADS
    scale = math.log2(math.e) / math.sqrt(HEAD_SIZE)
    usable = iota((keys, share * tokens), 0) < target_length[t]
    total = jnp.zeros((1, tokens), f32)
    for g in range(KEY_VALUE_HEADS):
        k = states_ref[0, :, g * HEAD_SIZE : (g + 1) * HEAD_SIZE]
        v = states_ref[0, :, width + g * HEAD_SIZE : width + (g + 1) * HEAD_SIZE]
        q = jnp.concatenate(
            [
                queries_ref[0, :, h * HEAD_SIZE : (h + 1) * HEAD_SIZE]
                for h in range(g * share, (g + 1) * share)
            ],
            axis=0,
        )
        scores = jnp.where(usable, dot_nt(k, q), MASKED)
        weights = jnp.exp2((scores - jnp.max(scores, axis=0, keepdims=True)) * scale)
        read = dot_nt(v, readout_ref[g * share : (g + 1) * share, :])
        read = jnp.concatenate(
            [jnp.broadcast_to(read[:, h : h + 1], (keys, tokens)) for h in range(share)], axis=1
        )
        ratio = jnp.sum(weights * read, axis=0, keepdims=True) / jnp.sum(
            weights, axis=0, keepdims=True
        )
        for h in range(share):
            total = total + ratio[:, h * tokens : (h + 1) * tokens]
    source = tokens // slots
    lane = iota((slots, tokens), 1)
    length = length_ref[0]
    wanted = (lane // source == iota((slots, tokens), 0)) & (lane % source < length)
    out_ref[0] = jnp.where(wanted, jnp.broadcast_to(total, (slots, tokens)), 0.0) / length.astype(f32)


def channel_kernel(
    rows,
    share,
    at_ref,
    arrived_ref,
    queries_ref,
    direct_ref,
    length_ref,
    row_ref,
    pick_ref,
    weight_ref,
    mine_ref,
    out_ref,
    keys_ref,
    read_ref,
):
    targets = queries_ref.shape[0]
    columns = queries_ref.shape[3]
    slots = direct_ref.shape[1]
    peers = out_ref.shape[0]
    keys = keys_ref.shape[2] // slots
    body = rows * keys
    heads = KEY_VALUE_HEADS * share
    per = arrived_ref.shape[1] // HEAD_SIZE
    scale = math.log2(math.e) / math.sqrt(HEAD_SIZE)
    lane = iota((slots, LANES), 1)
    position = iota((keys, slots, columns), 0)
    gathered = jnp.zeros((slots, LANES), f32)
    for t in range(targets):
        for s in range(slots):
            start = pl.multiple_of(at_ref[0, t * slots + s], keys)
            for j in range(KEY_VALUE_HEADS // per):
                key = arrived_ref[pl.ds(start + j * body, keys), :].astype(f32)
                for g in range(per):
                    keys_ref[t, j * per + g, pl.ds(s, keys, stride=slots), :] = key[
                        :, g * HEAD_SIZE : (g + 1) * HEAD_SIZE
                    ]
            start = pl.multiple_of(at_ref[1, t * slots + s], keys)
            across = pl.multiple_of(at_ref[2, t * slots + s], LANES)
            read_ref[t, pl.ds(s, keys, stride=slots), :] = arrived_ref[
                pl.ds(start, keys), pl.ds(across, LANES)
            ].astype(f32)
        read = read_ref[t]
        read = read + pltpu.roll(read, LANES - heads, 1)
        usable = position < jnp.concatenate([length_ref[t]] * (columns // LANES), axis=1)[None]
        total = jnp.zeros((slots, columns), f32)
        for g in range(KEY_VALUE_HEADS):
            scores = dot_nn(keys_ref[t, g].astype(bf16), queries_ref[t, g])
            scores = jnp.where(usable, scores.reshape(keys, slots, columns), MASKED)
            weights = jnp.exp2((scores - jnp.max(scores, axis=0, keepdims=True)) * scale)
            pick = pick_ref[t] + g * share
            value = jnp.concatenate(
                [
                    jnp.take_along_axis(read[i * slots : (i + 1) * slots, :], pick, axis=1)
                    for i in range(keys)
                ],
                axis=0,
            )
            value = jnp.concatenate([value] * (columns // LANES), axis=1)
            value = value.reshape(keys, slots, columns)
            total = total + jnp.sum(weights * value, axis=0) / jnp.sum(weights, axis=0)
        total = total * weight_ref[t : t + 1, :]
        combined = direct_ref[t]
        for i in range(columns // LANES):
            combined = combined + total[:, i * LANES : (i + 1) * LANES]
        combined = jnp.sum(combined, axis=1, keepdims=True)
        gathered = gathered + jnp.where(row_ref[t] == lane, combined, 0.0)
    gathered = jnp.sum(gathered, axis=0, keepdims=True)
    at = iota((peers, LANES), 1) - iota((peers, LANES), 0) * rows
    out = jnp.zeros((peers, LANES), f32)
    for r in range(rows):
        sent = jnp.sum(jnp.where(at == r, gathered, 0.0), axis=1, keepdims=True)
        out = out + jnp.where(mine_ref[...] == r, sent, 0.0)
    out_ref[...] = out


def on_device(
    candidate_queries,
    target_states,
    target_queries,
    candidate_states,
    target_length,
    candidate_length,
    candidate_row,
    direct_readout,
    channel_readout,
    *,
    peers,
):
    targets, slots, keys, query_width = candidate_queries.shape
    tokens = target_queries.shape[1]
    candidates = candidate_states.shape[0]
    width = candidate_states.shape[2] // 2
    heads = query_width // HEAD_SIZE
    share = heads // KEY_VALUE_HEADS
    rows = candidates // peers
    columns = share * tokens
    assert slots == SUBLANES and keys == 2 * SUBLANES and slots * keys == LANES
    assert 4 * heads == LANES and width == 4 * LANES and rows <= 4 and candidates <= LANES

    body = rows * keys
    chunk = 2 * body + keys
    hbm = pl.BlockSpec(memory_space=pltpu.HBM)
    packed = pl.pallas_call(
        functools.partial(pack_kernel, rows, keys),
        out_shape=jax.ShapeDtypeStruct((peers, chunk, width // 2), bf16),
        in_specs=[hbm, hbm],
        out_specs=hbm,
        scratch_shapes=[
            pltpu.VMEM((peers, body, width), bf16),
            pltpu.VMEM((heads, HEAD_SIZE), bf16),
            pltpu.VMEM((peers, chunk, width // 2), bf16),
            pltpu.SemaphoreType.DMA((7,)),
        ],
        compiler_params=pltpu.CompilerParams(vmem_limit_bytes=16 * 2**20),
        name="pack",
    )(
        pltpu.with_memory_space_constraint(
            candidate_states.reshape(peers, body, 2 * width), pltpu.HBM
        ),
        pltpu.with_memory_space_constraint(channel_readout.reshape(heads, HEAD_SIZE), pltpu.HBM),
    )
    arrived = lax.all_to_all(packed, "dp", split_axis=0, concat_axis=0, tiled=True)

    length_lanes = jnp.broadcast_to(candidate_length[:, :, None], (targets, slots, LANES))
    row_lanes = jnp.broadcast_to(candidate_row[:, :, None], (targets, slots, LANES))
    flat = candidate_row.reshape(candidates)
    at = jnp.stack(
        [
            flat // rows * chunk + flat % rows * keys,
            flat // rows * chunk + 2 * body,
            flat % rows // 2 * LANES,
        ]
    )
    direct, place = pl.pallas_call(
        direct_kernel,
        out_shape=(
            jax.ShapeDtypeStruct((targets, slots, slots * keys), f32),
            pltpu.SMEM(at.shape, jnp.int32),
        ),
        grid_spec=pltpu.PrefetchScalarGridSpec(
            num_scalar_prefetch=2,
            grid=(targets,),
            in_specs=[
                pl.BlockSpec((1, slots * keys, query_width), lambda t, n, a: (t, 0, 0)),
                pl.BlockSpec((1, tokens, 2 * width), lambda t, n, a: (t, 0, 0)),
                pl.BlockSpec((heads, HEAD_SIZE), lambda t, n, a: (0, 0)),
                pl.BlockSpec((1, slots, LANES), lambda t, n, a: (t, 0, 0)),
            ],
            out_specs=(
                pl.BlockSpec((1, slots, slots * keys), lambda t, n, a: (t, 0, 0)),
                pl.BlockSpec(memory_space=pltpu.SMEM),
            ),
        ),
        compiler_params=pltpu.CompilerParams(vmem_limit_bytes=32 * 2**20),
        cost_estimate=pl.CostEstimate(
            flops=4 * candidate_queries.size * tokens,
            bytes_accessed=2 * candidate_queries.size,
            transcendentals=0,
        ),
        name="direct",
    )(
        target_length,
        at,
        candidate_queries.reshape(targets, slots * keys, query_width),
        target_states,
        direct_readout.reshape(heads, HEAD_SIZE),
        length_lanes,
    )

    queries = target_queries.reshape(targets, tokens, KEY_VALUE_HEADS, share, HEAD_SIZE)
    queries = queries.transpose(0, 2, 4, 1, 3).reshape(
        targets, KEY_VALUE_HEADS, HEAD_SIZE, columns
    )
    lanes = jnp.arange(LANES, dtype=jnp.int32)
    pick = lanes % share + row_lanes % rows % 2 * (2 * heads)
    token = jnp.arange(columns, dtype=jnp.int32)[None, :] // share
    count = target_length[:, None]
    weight = jnp.where(token < count, 1.0 / count.astype(f32), 0.0)
    mine = (lanes - lax.axis_index("dp").astype(jnp.int32) * rows)[None, :]
    vmem = pl.BlockSpec(memory_space=pltpu.VMEM)
    smem = pl.BlockSpec(memory_space=pltpu.SMEM)
    outgoing = pl.pallas_call(
        functools.partial(channel_kernel, rows, share),
        out_shape=jax.ShapeDtypeStruct((peers, LANES), f32),
        in_specs=[smem] + [vmem] * 8,
        out_specs=vmem,
        scratch_shapes=[
            pltpu.VMEM((targets, KEY_VALUE_HEADS, slots * keys, HEAD_SIZE), f32),
            pltpu.VMEM((targets, slots * keys, LANES), f32),
        ],
        compiler_params=pltpu.CompilerParams(vmem_limit_bytes=32 * 2**20),
        name="channel",
    )(
        place,
        arrived.reshape(peers * chunk, width // 2),
        queries,
        direct,
        length_lanes,
        row_lanes,
        pick,
        weight,
        mine,
    )
    returned = lax.all_to_all(outgoing, "dp", split_axis=0, concat_axis=0, tiled=True)
    return jnp.sum(returned, axis=0)[:candidates]


def solution(mesh):
    in_specs = (
        P(("group", "dp"), None, None, None),
        P(("group", "dp"), None, None),
        P(("group", "dp"), None, None),
        P(("group", "dp"), None, None),
        P(("group", "dp")),
        P(("group", "dp"), None),
        P(("group", "dp"), None),
        P(),
        P(),
    )
    out_specs = P(("group", "dp"))
    return jax.shard_map(
        functools.partial(on_device, peers=mesh.shape["dp"]),
        mesh=mesh,
        in_specs=in_specs,
        out_specs=out_specs,
        check_vma=False,
    )
```

```python
import functools
import math

import jax
import jax.numpy as jnp
from jax import lax
from jax.experimental import pallas as pl
from jax.experimental.pallas import tpu as pltpu
from jax.sharding import PartitionSpec as P

KEY_VALUE_HEADS = 4
HEAD_SIZE = 128
LANES = 128
SUBLANES = 8
MASKED = -1e30
PACKED = 4
KEY_PARTS = 2

bf16 = jnp.bfloat16
f32 = jnp.float32


def dot_nt(a, b):
    return lax.dot_general(a, b, (((1,), (1,)), ((), ())), preferred_element_type=f32)


def dot_nn(a, b):
    return lax.dot_general(a, b, (((1,), (0,)), ((), ())), preferred_element_type=f32)


def iota(shape, axis):
    return lax.broadcasted_iota(jnp.int32, shape, axis)


def keys_kernel(states_ref, out_ref, held_ref, sems):
    peers, _, width = out_ref.shape
    parts = sems.shape[1]
    step = peers // parts
    loads, sends = [], []
    for i in range(parts):
        at = pl.ds(i * step, step)
        loads.append(
            pltpu.make_async_copy(states_ref.at[at, :, :width], held_ref.at[at], sems.at[0, i])
        )
        sends.append(pltpu.make_async_copy(held_ref.at[at], out_ref.at[at], sems.at[1, i]))
        loads[i].start()
    for i in range(parts):
        loads[i].wait()
        sends[i].start()
    for copy in sends:
        copy.wait()


def value_kernel(rows, keys, values_ref, readout_ref, factor_ref, first_ref, read_ref):
    peers, body, width = values_ref.shape
    share = readout_ref.shape[0] // KEY_VALUE_HEADS
    wide = LANES // KEY_VALUE_HEADS
    blocks = []
    for g in range(KEY_VALUE_HEADS):
        block = jnp.concatenate(
            [readout_ref[g * share : (g + 1) * share, :].astype(f32)] * (wide // share), axis=0
        )
        none = jnp.zeros_like(block)
        blocks.append(
            jnp.concatenate([block if i == g else none for i in range(KEY_VALUE_HEADS)], axis=1)
        )
    spread = jnp.concatenate(blocks, axis=0).astype(bf16)
    read_ref[...] = dot_nt(values_ref[...].reshape(peers * body, width), spread)
    part = iota((PACKED, LANES), 1) % wide // share
    first_key = (iota((PACKED, LANES), 0) == 0) & (part == 0)
    if rows < PACKED:
        factor_ref[...] = jnp.zeros_like(factor_ref)
    first_ref[...] = jnp.zeros_like(first_ref)
    for p in range(peers):
        for r in range(rows):
            start = p * body + r * keys
            value = read_ref[pl.ds(start, PACKED, stride=PACKED), :]
            for i in range(1, PACKED):
                value = jnp.where(part == i, read_ref[pl.ds(start + i, PACKED, stride=PACKED), :], value)
            first = read_ref[start : start + 1, :]
            factor_ref[p, pl.ds(r, PACKED, stride=PACKED), :] = jnp.where(first_key, 1.0, value - first)
            first_ref[p, r : r + 1, :] = jnp.where(part[:1] == 0, first, 0.0)


def direct_kernel(
    target_length, at_ref, queries_ref, states_ref, readout_ref, length_ref, out_ref, place_ref
):
    t = pl.program_id(0)

    @pl.when(t == 0)
    def _():
        for i in range(at_ref.shape[0]):
            for j in range(at_ref.shape[1]):
                place_ref[i, j] = at_ref[i, j]

    keys = states_ref.shape[1]
    width = states_ref.shape[2] // 2
    tokens = queries_ref.shape[1]
    slots = length_ref.shape[1]
    heads = readout_ref.shape[0]
    share = heads // KEY_VALUE_HEADS
    scale = math.log2(math.e) / math.sqrt(HEAD_SIZE)
    usable = iota((keys, share * tokens), 0) < target_length[t]
    total = jnp.zeros((1, tokens), f32)
    for g in range(KEY_VALUE_HEADS):
        k = states_ref[0, :, g * HEAD_SIZE : (g + 1) * HEAD_SIZE]
        v = states_ref[0, :, width + g * HEAD_SIZE : width + (g + 1) * HEAD_SIZE]
        q = jnp.concatenate(
            [
                queries_ref[0, :, h * HEAD_SIZE : (h + 1) * HEAD_SIZE]
                for h in range(g * share, (g + 1) * share)
            ],
            axis=0,
        )
        scores = jnp.where(usable, dot_nt(k, q), MASKED)
        weights = jnp.exp2((scores - jnp.max(scores, axis=0, keepdims=True)) * scale)
        read = dot_nt(v, readout_ref[g * share : (g + 1) * share, :])
        read = jnp.concatenate(
            [jnp.broadcast_to(read[:, h : h + 1], (keys, tokens)) for h in range(share)], axis=1
        )
        ratio = jnp.sum(weights * read, axis=0, keepdims=True) / jnp.sum(
            weights, axis=0, keepdims=True
        )
        for h in range(share):
            total = total + ratio[:, h * tokens : (h + 1) * tokens]
    source = tokens // slots
    lane = iota((slots, tokens), 1)
    length = length_ref[0]
    wanted = (lane // source == iota((slots, tokens), 0)) & (lane % source < length)
    total = jnp.where(wanted, jnp.broadcast_to(total, (slots, tokens)), 0.0)
    total = jnp.sum(total, axis=1, keepdims=True) / length.astype(f32)
    out_ref[0] = jnp.where(lane == 0, total, 0.0)


def halves(a, b, bit, lane):
    upper = lane // bit % 2 == 1
    moved = jnp.where(upper, a, b)
    if 2 * bit == LANES:
        moved = pltpu.roll(moved, bit, 1)
    else:
        moved = jnp.take_along_axis(moved, lane + jnp.where(upper, -bit, bit), axis=1)
    return jnp.where(upper, b, a) + moved


def channel_kernel(
    rows,
    place_ref,
    arrived_ref,
    queries_ref,
    direct_ref,
    length_ref,
    weight_ref,
    out_ref,
    keys_ref,
    pooled_ref,
):
    targets = queries_ref.shape[0]
    columns = queries_ref.shape[3]
    slots = direct_ref.shape[1]
    peers = out_ref.shape[0]
    keys = keys_ref.shape[2] // slots
    wide = LANES // KEY_VALUE_HEADS
    share = wide // PACKED
    scale = math.log2(math.e) / math.sqrt(HEAD_SIZE)
    position = iota((keys, slots, columns), 0)
    lane = iota((slots, LANES), 1)
    for t in range(targets):
        for s in range(slots):
            start = pl.multiple_of(place_ref[0, t * slots + s], keys)
            key = arrived_ref[pl.ds(start, keys), :].astype(f32)
            for g in range(KEY_VALUE_HEADS):
                keys_ref[t, g, pl.ds(s, keys, stride=slots), :] = key[
                    :, g * HEAD_SIZE : (g + 1) * HEAD_SIZE
                ]
        usable = position < jnp.concatenate([length_ref[t]] * (columns // LANES), axis=1)[None]
        parts = []
        for g in range(KEY_VALUE_HEADS):
            scores = dot_nn(keys_ref[t, g].astype(bf16), queries_ref[t, g])
            scores = jnp.where(usable, scores.reshape(keys, slots, columns), MASKED)
            weights = jnp.exp2((scores - jnp.max(scores, axis=0, keepdims=True)) * scale)
            weights = weights * (weight_ref[t : t + 1, :] / jnp.sum(weights, axis=0))[None]
            part = weights[:, :, :LANES]
            for i in range(1, columns // LANES):
                part = part + weights[:, :, i * LANES : (i + 1) * LANES]
            parts.append(part)
        for i in range(keys // PACKED):
            part = []
            for k in range(i * PACKED, (i + 1) * PACKED):
                low = halves(parts[0][k], parts[2][k], 2 * wide, lane)
                high = halves(parts[1][k], parts[3][k], 2 * wide, lane)
                part.append(halves(low, high, wide, lane))
            low = halves(part[0], part[2], 2 * share, lane)
            high = halves(part[1], part[3], 2 * share, lane)
            part = halves(low, high, share, lane)
            if i == 0:
                part = jnp.where(lane % wide < share, direct_ref[t], part)
            start = (t * (keys // PACKED) + i) * slots
            pooled_ref[start : start + slots, :] = part
    if rows < PACKED:
        out_ref[...] = jnp.zeros_like(out_ref)
    for p in range(peers):
        for r in range(rows):
            out_ref[p, pl.ds(r, PACKED, stride=PACKED), :] = pooled_ref[
                pl.ds(place_ref[1, p * rows + r], PACKED, stride=slots), :
            ]


def finish_kernel(rows, returned_ref, factor_ref, first_ref, out_ref):
    total = returned_ref[...] * factor_ref[...]
    total = total[:, :SUBLANES] + total[:, SUBLANES:] + first_ref[...]
    total = jnp.sum(total, axis=2, keepdims=True)
    shape = (total.shape[0], SUBLANES, LANES)
    at = iota(shape, 0) * rows + iota(shape, 1) % PACKED
    total = jnp.where((iota(shape, 2) == at) & (iota(shape, 1) % PACKED < rows), total, 0.0)
    total = jnp.sum(jnp.sum(total, axis=0), axis=0, keepdims=True)
    out_ref[...] = total[:, : out_ref.shape[1]]


def on_device(
    candidate_queries,
    target_states,
    target_queries,
    candidate_states,
    target_length,
    candidate_length,
    candidate_row,
    direct_readout,
    channel_readout,
    *,
    peers,
):
    targets, slots, keys, query_width = candidate_queries.shape
    tokens = target_queries.shape[1]
    candidates = candidate_states.shape[0]
    width = candidate_states.shape[2] // 2
    heads = query_width // HEAD_SIZE
    share = heads // KEY_VALUE_HEADS
    rows = candidates // peers
    columns = share * tokens
    assert slots == SUBLANES and keys == 2 * SUBLANES and slots * keys == LANES
    assert 4 * heads == LANES and width == 4 * LANES and rows <= 4 and candidates <= LANES

    body = rows * keys
    vmem = pl.BlockSpec(memory_space=pltpu.VMEM)
    smem = pl.BlockSpec(memory_space=pltpu.SMEM)
    assert keys == PACKED * PACKED and rows <= PACKED and share == LANES // KEY_VALUE_HEADS // PACKED
    hbm = pl.BlockSpec(memory_space=pltpu.HBM)
    sent = pl.pallas_call(
        keys_kernel,
        out_shape=jax.ShapeDtypeStruct((peers, body, width), bf16),
        in_specs=[hbm],
        out_specs=hbm,
        scratch_shapes=[
            pltpu.VMEM((peers, body, width), bf16),
            pltpu.SemaphoreType.DMA((2, KEY_PARTS)),
        ],
        compiler_params=pltpu.CompilerParams(vmem_limit_bytes=16 * 2**20),
        name="keys",
    )(pltpu.with_memory_space_constraint(candidate_states.reshape(peers, body, 2 * width), pltpu.HBM))
    arrived = lax.all_to_all(sent, "dp", split_axis=0, concat_axis=0, tiled=True)

    step = max(1, peers // 4)
    factor, first = pl.pallas_call(
        functools.partial(value_kernel, rows, keys),
        out_shape=(
            jax.ShapeDtypeStruct((peers, keys, LANES), f32),
            jax.ShapeDtypeStruct((peers, SUBLANES, LANES), f32),
        ),
        grid=(peers // step,),
        in_specs=[
            pl.BlockSpec((step, body, width), lambda i: (i, 0, 1)),
            pl.BlockSpec((heads, HEAD_SIZE), lambda i: (0, 0)),
        ],
        out_specs=(
            pl.BlockSpec((step, keys, LANES), lambda i: (i, 0, 0)),
            pl.BlockSpec((step, SUBLANES, LANES), lambda i: (i, 0, 0)),
        ),
        scratch_shapes=[pltpu.VMEM((step * body, LANES), f32)],
        compiler_params=pltpu.CompilerParams(vmem_limit_bytes=16 * 2**20),
        cost_estimate=pl.CostEstimate(
            flops=2 * LANES * width * candidates * keys,
            bytes_accessed=candidate_states.size,
            transcendentals=0,
        ),
        name="value",
    )(
        candidate_states.reshape(peers, body, 2 * width),
        channel_readout.reshape(heads, HEAD_SIZE),
    )

    length_lanes = jnp.broadcast_to(candidate_length[:, :, None], (targets, slots, LANES))
    flat = candidate_row.reshape(candidates)
    pair = jnp.arange(candidates, dtype=jnp.int32)
    start = pair // slots * (slots * PACKED) + pair % slots
    start = jnp.sum(jnp.where(flat[None, :] == pair[:, None], start[None, :], 0), axis=1)
    at = jnp.stack([flat * keys, start])
    direct, place = pl.pallas_call(
        direct_kernel,
        out_shape=(
            jax.ShapeDtypeStruct((targets, slots, slots * keys), f32),
            pltpu.SMEM(at.shape, jnp.int32),
        ),
        grid_spec=pltpu.PrefetchScalarGridSpec(
            num_scalar_prefetch=2,
            grid=(targets,),
            in_specs=[
                pl.BlockSpec((1, slots * keys, query_width), lambda t, n, a: (t, 0, 0)),
                pl.BlockSpec((1, tokens, 2 * width), lambda t, n, a: (t, 0, 0)),
                pl.BlockSpec((heads, HEAD_SIZE), lambda t, n, a: (0, 0)),
                pl.BlockSpec((1, slots, LANES), lambda t, n, a: (t, 0, 0)),
            ],
            out_specs=(
                pl.BlockSpec((1, slots, slots * keys), lambda t, n, a: (t, 0, 0)),
                pl.BlockSpec(memory_space=pltpu.SMEM),
            ),
        ),
        compiler_params=pltpu.CompilerParams(vmem_limit_bytes=32 * 2**20),
        cost_estimate=pl.CostEstimate(
            flops=4 * candidate_queries.size * tokens,
            bytes_accessed=2 * candidate_queries.size,
            transcendentals=0,
        ),
        name="direct",
    )(
        target_length,
        at,
        candidate_queries.reshape(targets, slots * keys, query_width),
        target_states,
        direct_readout.reshape(heads, HEAD_SIZE),
        length_lanes,
    )

    queries = target_queries.reshape(targets, tokens, KEY_VALUE_HEADS, share, HEAD_SIZE)
    queries = queries.transpose(0, 2, 4, 1, 3).reshape(
        targets, KEY_VALUE_HEADS, HEAD_SIZE, columns
    )
    token = jnp.arange(columns, dtype=jnp.int32)[None, :] // share
    count = target_length[:, None]
    weight = jnp.where(token < count, 1.0 / count.astype(f32), 0.0)
    outgoing = pl.pallas_call(
        functools.partial(channel_kernel, rows),
        out_shape=jax.ShapeDtypeStruct((peers, keys, LANES), f32),
        in_specs=[smem] + [vmem] * 5,
        out_specs=vmem,
        scratch_shapes=[
            pltpu.VMEM((targets, KEY_VALUE_HEADS, slots * keys, HEAD_SIZE), f32),
            pltpu.VMEM((targets * slots * PACKED, LANES), f32),
        ],
        compiler_params=pltpu.CompilerParams(vmem_limit_bytes=32 * 2**20),
        name="channel",
    )(
        place,
        arrived.reshape(peers * body, width),
        queries,
        direct,
        length_lanes,
        weight,
    )
    returned = lax.all_to_all(outgoing, "dp", split_axis=0, concat_axis=0, tiled=True)
    result = pl.pallas_call(
        functools.partial(finish_kernel, rows),
        out_shape=jax.ShapeDtypeStruct((1, candidates), f32),
        in_specs=[vmem] * 3,
        out_specs=vmem,
        compiler_params=pltpu.CompilerParams(vmem_limit_bytes=16 * 2**20),
        name="finish",
    )(returned, factor, first)
    return result.reshape(candidates)


def solution(mesh):
    in_specs = (
        P(("group", "dp"), None, None, None),
        P(("group", "dp"), None, None),
        P(("group", "dp"), None, None),
        P(("group", "dp"), None, None),
        P(("group", "dp")),
        P(("group", "dp"), None),
        P(("group", "dp"), None),
        P(),
        P(),
    )
    out_specs = P(("group", "dp"))
    return jax.shard_map(
        functools.partial(on_device, peers=mesh.shape["dp"]),
        mesh=mesh,
        in_specs=in_specs,
        out_specs=out_specs,
        check_vma=False,
    )
```

```python
import functools
import math

import jax
import jax.numpy as jnp
from jax import lax
from jax.experimental import pallas as pl
from jax.experimental.pallas import tpu as pltpu
from jax.sharding import PartitionSpec as P

KEY_VALUE_HEADS = 4
HEAD_SIZE = 128
LANES = 128
SUBLANES = 8
MASKED = -1e30
PACKED = 4
KEY_PARTS = 4

bf16 = jnp.bfloat16
f32 = jnp.float32


def dot_nt(a, b):
    return lax.dot_general(a, b, (((1,), (1,)), ((), ())), preferred_element_type=f32)


def dot_nn(a, b):
    return lax.dot_general(a, b, (((1,), (0,)), ((), ())), preferred_element_type=f32)


def iota(shape, axis):
    return lax.broadcasted_iota(jnp.int32, shape, axis)


def keys_kernel(states_ref, out_ref, held_ref, sems):
    peers, _, width = out_ref.shape
    parts = sems.shape[1]
    step = peers // parts
    loads, sends = [], []
    for i in range(parts):
        at = pl.ds(i * step, step)
        loads.append(
            pltpu.make_async_copy(states_ref.at[at, :, :width], held_ref.at[at], sems.at[0, i])
        )
        sends.append(pltpu.make_async_copy(held_ref.at[at], out_ref.at[at], sems.at[1, i]))
        loads[i].start()
    for i in range(parts):
        loads[i].wait()
        sends[i].start()
    for copy in sends:
        copy.wait()


def value_kernel(rows, keys, values_ref, readout_ref, factor_ref, first_ref, read_ref):
    peers, body, width = values_ref.shape
    share = readout_ref.shape[0] // KEY_VALUE_HEADS
    wide = LANES // KEY_VALUE_HEADS
    blocks = []
    for g in range(KEY_VALUE_HEADS):
        block = jnp.concatenate(
            [readout_ref[g * share : (g + 1) * share, :].astype(f32)] * (wide // share), axis=0
        )
        none = jnp.zeros_like(block)
        blocks.append(
            jnp.concatenate([block if i == g else none for i in range(KEY_VALUE_HEADS)], axis=1)
        )
    spread = jnp.concatenate(blocks, axis=0).astype(bf16)
    read_ref[...] = dot_nt(values_ref[...].reshape(peers * body, width), spread)
    part = iota((PACKED, LANES), 1) % wide // share
    first_key = (iota((PACKED, LANES), 0) == 0) & (part == 0)
    if rows < PACKED:
        factor_ref[...] = jnp.zeros_like(factor_ref)
    first_ref[...] = jnp.zeros_like(first_ref)
    for p in range(peers):
        for r in range(rows):
            start = p * body + r * keys
            value = read_ref[pl.ds(start, PACKED, stride=PACKED), :]
            for i in range(1, PACKED):
                value = jnp.where(part == i, read_ref[pl.ds(start + i, PACKED, stride=PACKED), :], value)
            first = read_ref[start : start + 1, :]
            factor_ref[p, pl.ds(r, PACKED, stride=PACKED), :] = jnp.where(first_key, 1.0, value - first)
            first_ref[p, r : r + 1, :] = jnp.where(part[:1] == 0, first, 0.0)


def direct_kernel(
    target_length, at_ref, queries_ref, states_ref, readout_ref, length_ref, out_ref, place_ref
):
    t = pl.program_id(0)

    @pl.when(t == 0)
    def _():
        for i in range(at_ref.shape[0]):
            for j in range(at_ref.shape[1]):
                place_ref[i, j] = at_ref[i, j]

    keys = states_ref.shape[1]
    width = states_ref.shape[2] // 2
    tokens = queries_ref.shape[1]
    slots = length_ref.shape[1]
    heads = readout_ref.shape[0]
    share = heads // KEY_VALUE_HEADS
    scale = math.log2(math.e) / math.sqrt(HEAD_SIZE)
    usable = iota((keys, share * tokens), 0) < target_length[t]
    total = jnp.zeros((1, tokens), f32)
    for g in range(KEY_VALUE_HEADS):
        k = states_ref[0, :, g * HEAD_SIZE : (g + 1) * HEAD_SIZE]
        v = states_ref[0, :, width + g * HEAD_SIZE : width + (g + 1) * HEAD_SIZE]
        q = jnp.concatenate(
            [
                queries_ref[0, :, h * HEAD_SIZE : (h + 1) * HEAD_SIZE]
                for h in range(g * share, (g + 1) * share)
            ],
            axis=0,
        )
        scores = jnp.where(usable, dot_nt(k, q), MASKED)
        weights = jnp.exp2((scores - jnp.max(scores, axis=0, keepdims=True)) * scale)
        read = dot_nt(v, readout_ref[g * share : (g + 1) * share, :])
        read = jnp.concatenate(
            [jnp.broadcast_to(read[:, h : h + 1], (keys, tokens)) for h in range(share)], axis=1
        )
        ratio = jnp.sum(weights * read, axis=0, keepdims=True) / jnp.sum(
            weights, axis=0, keepdims=True
        )
        for h in range(share):
            total = total + ratio[:, h * tokens : (h + 1) * tokens]
    source = tokens // slots
    lane = iota((slots, tokens), 1)
    length = length_ref[0]
    wanted = (lane // source == iota((slots, tokens), 0)) & (lane % source < length)
    total = jnp.where(wanted, jnp.broadcast_to(total, (slots, tokens)), 0.0)
    total = jnp.sum(total, axis=1, keepdims=True) / length.astype(f32)
    out_ref[0] = jnp.where(lane == 0, total, 0.0)


def halves(a, b, bit, lane):
    upper = lane // bit % 2 == 1
    moved = jnp.where(upper, a, b)
    if 2 * bit == LANES:
        moved = pltpu.roll(moved, bit, 1)
    else:
        moved = jnp.take_along_axis(moved, lane + jnp.where(upper, -bit, bit), axis=1)
    return jnp.where(upper, b, a) + moved


def channel_kernel(
    rows,
    place_ref,
    arrived_ref,
    queries_ref,
    direct_ref,
    length_ref,
    weight_ref,
    out_ref,
    keys_ref,
    pooled_ref,
):
    targets = queries_ref.shape[0]
    columns = queries_ref.shape[3]
    slots = direct_ref.shape[1]
    peers = out_ref.shape[0]
    keys = keys_ref.shape[2] // slots
    wide = LANES // KEY_VALUE_HEADS
    share = wide // PACKED
    scale = math.log2(math.e) / math.sqrt(HEAD_SIZE)
    position = iota((keys, slots, columns), 0)
    lane = iota((slots, LANES), 1)
    for t in range(targets):
        for s in range(slots):
            start = pl.multiple_of(place_ref[0, t * slots + s], keys)
            key = arrived_ref[pl.ds(start, keys), :].astype(f32)
            for g in range(KEY_VALUE_HEADS):
                keys_ref[t, g, pl.ds(s, keys, stride=slots), :] = key[
                    :, g * HEAD_SIZE : (g + 1) * HEAD_SIZE
                ]
        usable = position < jnp.concatenate([length_ref[t]] * (columns // LANES), axis=1)[None]
        parts = []
        for g in range(KEY_VALUE_HEADS):
            scores = dot_nn(keys_ref[t, g].astype(bf16), queries_ref[t, g])
            scores = jnp.where(usable, scores.reshape(keys, slots, columns), MASKED)
            weights = jnp.exp2((scores - jnp.max(scores, axis=0, keepdims=True)) * scale)
            weights = weights * (weight_ref[t : t + 1, :] / jnp.sum(weights, axis=0))[None]
            part = weights[:, :, :LANES]
            for i in range(1, columns // LANES):
                part = part + weights[:, :, i * LANES : (i + 1) * LANES]
            parts.append(part)
        for i in range(keys // PACKED):
            part = []
            for k in range(i * PACKED, (i + 1) * PACKED):
                low = halves(parts[0][k], parts[2][k], 2 * wide, lane)
                high = halves(parts[1][k], parts[3][k], 2 * wide, lane)
                part.append(halves(low, high, wide, lane))
            low = halves(part[0], part[2], 2 * share, lane)
            high = halves(part[1], part[3], 2 * share, lane)
            part = halves(low, high, share, lane)
            if i == 0:
                part = jnp.where(lane % wide < share, direct_ref[t], part)
            start = (t * (keys // PACKED) + i) * slots
            pooled_ref[start : start + slots, :] = part
    if rows < PACKED:
        out_ref[...] = jnp.zeros_like(out_ref)
    for p in range(peers):
        for r in range(rows):
            out_ref[p, pl.ds(r, PACKED, stride=PACKED), :] = pooled_ref[
                pl.ds(place_ref[1, p * rows + r], PACKED, stride=slots), :
            ]


def finish_kernel(rows, returned_ref, factor_ref, first_ref, out_ref):
    total = returned_ref[...] * factor_ref[...]
    total = total[:, :SUBLANES] + total[:, SUBLANES:] + first_ref[...]
    total = jnp.sum(total, axis=2, keepdims=True)
    shape = (total.shape[0], SUBLANES, LANES)
    at = iota(shape, 0) * rows + iota(shape, 1) % PACKED
    total = jnp.where((iota(shape, 2) == at) & (iota(shape, 1) % PACKED < rows), total, 0.0)
    total = jnp.sum(jnp.sum(total, axis=0), axis=0, keepdims=True)
    out_ref[...] = total[:, : out_ref.shape[1]]


def on_device(
    candidate_queries,
    target_states,
    target_queries,
    candidate_states,
    target_length,
    candidate_length,
    candidate_row,
    direct_readout,
    channel_readout,
    *,
    peers,
):
    targets, slots, keys, query_width = candidate_queries.shape
    tokens = target_queries.shape[1]
    candidates = candidate_states.shape[0]
    width = candidate_states.shape[2] // 2
    heads = query_width // HEAD_SIZE
    share = heads // KEY_VALUE_HEADS
    rows = candidates // peers
    columns = share * tokens
    assert slots == SUBLANES and keys == 2 * SUBLANES and slots * keys == LANES
    assert 4 * heads == LANES and width == 4 * LANES and rows <= 4 and candidates <= LANES

    body = rows * keys
    vmem = pl.BlockSpec(memory_space=pltpu.VMEM)
    smem = pl.BlockSpec(memory_space=pltpu.SMEM)
    assert keys == PACKED * PACKED and rows <= PACKED and share == LANES // KEY_VALUE_HEADS // PACKED
    hbm = pl.BlockSpec(memory_space=pltpu.HBM)
    sent = pl.pallas_call(
        keys_kernel,
        out_shape=jax.ShapeDtypeStruct((peers, body, width), bf16),
        in_specs=[hbm],
        out_specs=hbm,
        scratch_shapes=[
            pltpu.VMEM((peers, body, width), bf16),
            pltpu.SemaphoreType.DMA((2, KEY_PARTS)),
        ],
        compiler_params=pltpu.CompilerParams(vmem_limit_bytes=16 * 2**20),
        name="keys",
    )(pltpu.with_memory_space_constraint(candidate_states.reshape(peers, body, 2 * width), pltpu.HBM))
    arrived = lax.all_to_all(sent, "dp", split_axis=0, concat_axis=0, tiled=True)

    step = max(1, peers // 4)
    factor, first = pl.pallas_call(
        functools.partial(value_kernel, rows, keys),
        out_shape=(
            jax.ShapeDtypeStruct((peers, keys, LANES), f32),
            jax.ShapeDtypeStruct((peers, SUBLANES, LANES), f32),
        ),
        grid=(peers // step,),
        in_specs=[
            pl.BlockSpec((step, body, width), lambda i: (i, 0, 1)),
            pl.BlockSpec((heads, HEAD_SIZE), lambda i: (0, 0)),
        ],
        out_specs=(
            pl.BlockSpec((step, keys, LANES), lambda i: (i, 0, 0)),
            pl.BlockSpec((step, SUBLANES, LANES), lambda i: (i, 0, 0)),
        ),
        scratch_shapes=[pltpu.VMEM((step * body, LANES), f32)],
        compiler_params=pltpu.CompilerParams(vmem_limit_bytes=16 * 2**20),
        cost_estimate=pl.CostEstimate(
            flops=2 * LANES * width * candidates * keys,
            bytes_accessed=candidate_states.size,
            transcendentals=0,
        ),
        name="value",
    )(
        candidate_states.reshape(peers, body, 2 * width),
        channel_readout.reshape(heads, HEAD_SIZE),
    )

    length_lanes = jnp.broadcast_to(candidate_length[:, :, None], (targets, slots, LANES))
    flat = candidate_row.reshape(candidates)
    pair = jnp.arange(candidates, dtype=jnp.int32)
    start = pair // slots * (slots * PACKED) + pair % slots
    start = jnp.sum(jnp.where(flat[None, :] == pair[:, None], start[None, :], 0), axis=1)
    at = jnp.stack([flat * keys, start])
    direct, place = pl.pallas_call(
        direct_kernel,
        out_shape=(
            jax.ShapeDtypeStruct((targets, slots, slots * keys), f32),
            pltpu.SMEM(at.shape, jnp.int32),
        ),
        grid_spec=pltpu.PrefetchScalarGridSpec(
            num_scalar_prefetch=2,
            grid=(targets,),
            in_specs=[
                pl.BlockSpec((1, slots * keys, query_width), lambda t, n, a: (t, 0, 0)),
                pl.BlockSpec((1, tokens, 2 * width), lambda t, n, a: (t, 0, 0)),
                pl.BlockSpec((heads, HEAD_SIZE), lambda t, n, a: (0, 0)),
                pl.BlockSpec((1, slots, LANES), lambda t, n, a: (t, 0, 0)),
            ],
            out_specs=(
                pl.BlockSpec((1, slots, slots * keys), lambda t, n, a: (t, 0, 0)),
                pl.BlockSpec(memory_space=pltpu.SMEM),
            ),
        ),
        compiler_params=pltpu.CompilerParams(vmem_limit_bytes=32 * 2**20),
        cost_estimate=pl.CostEstimate(
            flops=4 * candidate_queries.size * tokens,
            bytes_accessed=2 * candidate_queries.size,
            transcendentals=0,
        ),
        name="direct",
    )(
        target_length,
        at,
        candidate_queries.reshape(targets, slots * keys, query_width),
        target_states,
        direct_readout.reshape(heads, HEAD_SIZE),
        length_lanes,
    )

    queries = target_queries.reshape(targets, tokens, KEY_VALUE_HEADS, share, HEAD_SIZE)
    queries = queries.transpose(0, 2, 4, 1, 3).reshape(
        targets, KEY_VALUE_HEADS, HEAD_SIZE, columns
    )
    token = jnp.arange(columns, dtype=jnp.int32)[None, :] // share
    count = target_length[:, None]
    weight = jnp.where(token < count, 1.0 / count.astype(f32), 0.0)
    direct, factor, first = lax.optimization_barrier((direct, factor, first))
    outgoing = pl.pallas_call(
        functools.partial(channel_kernel, rows),
        out_shape=jax.ShapeDtypeStruct((peers, keys, LANES), f32),
        in_specs=[smem] + [vmem] * 5,
        out_specs=vmem,
        scratch_shapes=[
            pltpu.VMEM((targets, KEY_VALUE_HEADS, slots * keys, HEAD_SIZE), f32),
            pltpu.VMEM((targets * slots * PACKED, LANES), f32),
        ],
        compiler_params=pltpu.CompilerParams(vmem_limit_bytes=32 * 2**20),
        name="channel",
    )(
        place,
        arrived.reshape(peers * body, width),
        queries,
        direct,
        length_lanes,
        weight,
    )
    returned = lax.all_to_all(outgoing, "dp", split_axis=0, concat_axis=0, tiled=True)
    result = pl.pallas_call(
        functools.partial(finish_kernel, rows),
        out_shape=jax.ShapeDtypeStruct((1, candidates), f32),
        in_specs=[vmem] * 3,
        out_specs=vmem,
        compiler_params=pltpu.CompilerParams(vmem_limit_bytes=16 * 2**20),
        name="finish",
    )(returned, factor, first)
    return result.reshape(candidates)


def solution(mesh):
    in_specs = (
        P(("group", "dp"), None, None, None),
        P(("group", "dp"), None, None),
        P(("group", "dp"), None, None),
        P(("group", "dp"), None, None),
        P(("group", "dp")),
        P(("group", "dp"), None),
        P(("group", "dp"), None),
        P(),
        P(),
    )
    out_specs = P(("group", "dp"))
    return jax.shard_map(
        functools.partial(on_device, peers=mesh.shape["dp"]),
        mesh=mesh,
        in_specs=in_specs,
        out_specs=out_specs,
        check_vma=False,
    )
```

```python
import functools
import math

import jax
import jax.numpy as jnp
from jax import lax
from jax.experimental import pallas as pl
from jax.experimental.pallas import tpu as pltpu
from jax.sharding import PartitionSpec as P

KEY_VALUE_HEADS = 4
HEAD_SIZE = 128
LANES = 128
SUBLANES = 8
MASKED = -1e30
PACKED = 4
KEY_PARTS = 4
OUT_FLIP = 3
BACK_FLIP = 3

bf16 = jnp.bfloat16
f32 = jnp.float32


def turned(i, count, flip):
    return ((i + count // 2) % count) ^ flip


def place_of(device, count, flip):
    return ((device ^ flip) + count // 2) % count


def dot_nt(a, b):
    return lax.dot_general(a, b, (((1,), (1,)), ((), ())), preferred_element_type=f32)


def dot_nn(a, b):
    return lax.dot_general(a, b, (((1,), (0,)), ((), ())), preferred_element_type=f32)


def iota(shape, axis):
    return lax.broadcasted_iota(jnp.int32, shape, axis)


def keys_kernel(states_ref, out_ref, held_ref, sems):
    peers, _, width = out_ref.shape
    parts = KEY_PARTS
    step = peers // parts
    loads, sends = [], []
    for i in range(parts):
        at = pl.ds(i * step, step)
        loads.append(
            pltpu.make_async_copy(states_ref.at[at, :, :width], held_ref.at[at], sems.at[0, i])
        )
        loads[i].start()
    for i in range(parts):
        loads[i].wait()
        size = step if OUT_FLIP == 0 else 1
        for j in range(i * step, (i + 1) * step, size):
            to = pl.ds(place_of(j, peers, OUT_FLIP), size)
            sends.append(
                pltpu.make_async_copy(held_ref.at[j : j + size], out_ref.at[to], sems.at[1, j // size])
            )
            sends[-1].start()
    for copy in sends:
        copy.wait()


def value_kernel(rows, keys, values_ref, readout_ref, factor_ref, first_ref, read_ref):
    peers, body, width = values_ref.shape
    share = readout_ref.shape[0] // KEY_VALUE_HEADS
    wide = LANES // KEY_VALUE_HEADS
    blocks = []
    for g in range(KEY_VALUE_HEADS):
        block = jnp.concatenate(
            [readout_ref[g * share : (g + 1) * share, :].astype(f32)] * (wide // share), axis=0
        )
        none = jnp.zeros_like(block)
        blocks.append(
            jnp.concatenate([block if i == g else none for i in range(KEY_VALUE_HEADS)], axis=1)
        )
    spread = jnp.concatenate(blocks, axis=0).astype(bf16)
    read_ref[...] = dot_nt(values_ref[...].reshape(peers * body, width), spread)
    part = iota((PACKED, LANES), 1) % wide // share
    first_key = (iota((PACKED, LANES), 0) == 0) & (part == 0)
    if rows < PACKED:
        factor_ref[...] = jnp.zeros_like(factor_ref)
    first_ref[...] = jnp.zeros_like(first_ref)
    for p in range(peers):
        to = p ^ BACK_FLIP
        for r in range(rows):
            start = p * body + r * keys
            value = read_ref[pl.ds(start, PACKED, stride=PACKED), :]
            for i in range(1, PACKED):
                value = jnp.where(part == i, read_ref[pl.ds(start + i, PACKED, stride=PACKED), :], value)
            first = read_ref[start : start + 1, :]
            factor_ref[to, pl.ds(r, PACKED, stride=PACKED), :] = jnp.where(first_key, 1.0, value - first)
            first_ref[to, r : r + 1, :] = jnp.where(part[:1] == 0, first, 0.0)


def direct_kernel(
    target_length, at_ref, queries_ref, states_ref, readout_ref, length_ref, out_ref, place_ref
):
    t = pl.program_id(0)

    @pl.when(t == 0)
    def _():
        for i in range(at_ref.shape[0]):
            for j in range(at_ref.shape[1]):
                place_ref[i, j] = at_ref[i, j]

    keys = states_ref.shape[1]
    width = states_ref.shape[2] // 2
    tokens = queries_ref.shape[1]
    slots = length_ref.shape[1]
    heads = readout_ref.shape[0]
    share = heads // KEY_VALUE_HEADS
    scale = math.log2(math.e) / math.sqrt(HEAD_SIZE)
    usable = iota((keys, share * tokens), 0) < target_length[t]
    total = jnp.zeros((1, tokens), f32)
    for g in range(KEY_VALUE_HEADS):
        k = states_ref[0, :, g * HEAD_SIZE : (g + 1) * HEAD_SIZE]
        v = states_ref[0, :, width + g * HEAD_SIZE : width + (g + 1) * HEAD_SIZE]
        q = jnp.concatenate(
            [
                queries_ref[0, :, h * HEAD_SIZE : (h + 1) * HEAD_SIZE]
                for h in range(g * share, (g + 1) * share)
            ],
            axis=0,
        )
        scores = jnp.where(usable, dot_nt(k, q), MASKED)
        weights = jnp.exp2((scores - jnp.max(scores, axis=0, keepdims=True)) * scale)
        read = dot_nt(v, readout_ref[g * share : (g + 1) * share, :])
        read = jnp.concatenate(
            [jnp.broadcast_to(read[:, h : h + 1], (keys, tokens)) for h in range(share)], axis=1
        )
        ratio = jnp.sum(weights * read, axis=0, keepdims=True) / jnp.sum(
            weights, axis=0, keepdims=True
        )
        for h in range(share):
            total = total + ratio[:, h * tokens : (h + 1) * tokens]
    source = tokens // slots
    lane = iota((slots, tokens), 1)
    length = length_ref[0]
    wanted = (lane // source == iota((slots, tokens), 0)) & (lane % source < length)
    total = jnp.where(wanted, jnp.broadcast_to(total, (slots, tokens)), 0.0)
    total = jnp.sum(total, axis=1, keepdims=True) / length.astype(f32)
    out_ref[0] = jnp.where(lane == 0, total, 0.0)


def halves(a, b, bit, lane):
    upper = lane // bit % 2 == 1
    moved = jnp.where(upper, a, b)
    if 2 * bit == LANES:
        moved = pltpu.roll(moved, bit, 1)
    else:
        moved = jnp.take_along_axis(moved, lane + jnp.where(upper, -bit, bit), axis=1)
    return jnp.where(upper, b, a) + moved


def channel_kernel(
    rows,
    place_ref,
    arrived_ref,
    queries_ref,
    direct_ref,
    length_ref,
    weight_ref,
    out_ref,
    keys_ref,
    pooled_ref,
):
    targets = queries_ref.shape[0]
    columns = queries_ref.shape[3]
    slots = direct_ref.shape[1]
    peers = out_ref.shape[0]
    keys = keys_ref.shape[2] // slots
    wide = LANES // KEY_VALUE_HEADS
    share = wide // PACKED
    scale = math.log2(math.e) / math.sqrt(HEAD_SIZE)
    position = iota((keys, slots, columns), 0)
    lane = iota((slots, LANES), 1)
    for t in range(targets):
        for s in range(slots):
            start = pl.multiple_of(place_ref[0, t * slots + s], keys)
            key = arrived_ref[pl.ds(start, keys), :].astype(f32)
            for g in range(KEY_VALUE_HEADS):
                keys_ref[t, g, pl.ds(s, keys, stride=slots), :] = key[
                    :, g * HEAD_SIZE : (g + 1) * HEAD_SIZE
                ]
        usable = position < jnp.concatenate([length_ref[t]] * (columns // LANES), axis=1)[None]
        parts = []
        for g in range(KEY_VALUE_HEADS):
            scores = dot_nn(keys_ref[t, g].astype(bf16), queries_ref[t, g])
            scores = jnp.where(usable, scores.reshape(keys, slots, columns), MASKED)
            weights = jnp.exp2((scores - jnp.max(scores, axis=0, keepdims=True)) * scale)
            weights = weights * (weight_ref[t : t + 1, :] / jnp.sum(weights, axis=0))[None]
            part = weights[:, :, :LANES]
            for i in range(1, columns // LANES):
                part = part + weights[:, :, i * LANES : (i + 1) * LANES]
            parts.append(part)
        for i in range(keys // PACKED):
            part = []
            for k in range(i * PACKED, (i + 1) * PACKED):
                low = halves(parts[0][k], parts[2][k], 2 * wide, lane)
                high = halves(parts[1][k], parts[3][k], 2 * wide, lane)
                part.append(halves(low, high, wide, lane))
            low = halves(part[0], part[2], 2 * share, lane)
            high = halves(part[1], part[3], 2 * share, lane)
            part = halves(low, high, share, lane)
            if i == 0:
                part = jnp.where(lane % wide < share, direct_ref[t], part)
            start = (t * (keys // PACKED) + i) * slots
            pooled_ref[start : start + slots, :] = part
    if rows < PACKED:
        out_ref[...] = jnp.zeros_like(out_ref)
    for i in range(peers):
        p = turned(i, peers, BACK_FLIP)
        for r in range(rows):
            out_ref[i, pl.ds(r, PACKED, stride=PACKED), :] = pooled_ref[
                pl.ds(place_ref[1, p * rows + r], PACKED, stride=slots), :
            ]


def finish_kernel(rows, returned_ref, factor_ref, first_ref, out_ref):
    total = returned_ref[...] * factor_ref[...]
    total = total[:, :SUBLANES] + total[:, SUBLANES:] + first_ref[...]
    total = jnp.sum(total, axis=2, keepdims=True)
    shape = (total.shape[0], SUBLANES, LANES)
    at = turned(iota(shape, 0), shape[0], BACK_FLIP) * rows + iota(shape, 1) % PACKED
    total = jnp.where((iota(shape, 2) == at) & (iota(shape, 1) % PACKED < rows), total, 0.0)
    total = jnp.sum(jnp.sum(total, axis=0), axis=0, keepdims=True)
    out_ref[...] = total[:, : out_ref.shape[1]]


def on_device(
    candidate_queries,
    target_states,
    target_queries,
    candidate_states,
    target_length,
    candidate_length,
    candidate_row,
    direct_readout,
    channel_readout,
    *,
    peers,
):
    targets, slots, keys, query_width = candidate_queries.shape
    tokens = target_queries.shape[1]
    candidates = candidate_states.shape[0]
    width = candidate_states.shape[2] // 2
    heads = query_width // HEAD_SIZE
    share = heads // KEY_VALUE_HEADS
    rows = candidates // peers
    columns = share * tokens
    assert slots == SUBLANES and keys == 2 * SUBLANES and slots * keys == LANES
    assert 4 * heads == LANES and width == 4 * LANES and rows <= 4 and candidates <= LANES

    body = rows * keys
    vmem = pl.BlockSpec(memory_space=pltpu.VMEM)
    smem = pl.BlockSpec(memory_space=pltpu.SMEM)
    assert keys == PACKED * PACKED and rows <= PACKED and share == LANES // KEY_VALUE_HEADS // PACKED
    hbm = pl.BlockSpec(memory_space=pltpu.HBM)
    sent = pl.pallas_call(
        keys_kernel,
        out_shape=jax.ShapeDtypeStruct((peers, body, width), bf16),
        in_specs=[hbm],
        out_specs=hbm,
        scratch_shapes=[
            pltpu.VMEM((peers, body, width), bf16),
            pltpu.SemaphoreType.DMA((2, KEY_PARTS if OUT_FLIP == 0 else peers)),
        ],
        compiler_params=pltpu.CompilerParams(vmem_limit_bytes=16 * 2**20),
        name="keys",
    )(pltpu.with_memory_space_constraint(candidate_states.reshape(peers, body, 2 * width), pltpu.HBM))
    assert peers % 16 == 0
    out_order = [turned(i, peers, OUT_FLIP) for i in range(peers)]
    back_order = [turned(i, peers, BACK_FLIP) for i in range(peers)]
    exchange = functools.partial(lax.all_to_all, axis_name="dp", split_axis=0, concat_axis=0, tiled=True)
    arrived = exchange(sent, axis_index_groups=[out_order])

    step = peers // 4
    half = 2
    factor, first = pl.pallas_call(
        functools.partial(value_kernel, rows, keys),
        out_shape=(
            jax.ShapeDtypeStruct((peers, keys, LANES), f32),
            jax.ShapeDtypeStruct((peers, SUBLANES, LANES), f32),
        ),
        grid=(peers // step,),
        in_specs=[
            pl.BlockSpec((step, body, width), lambda i: (i, 0, 1)),
            pl.BlockSpec((heads, HEAD_SIZE), lambda i: (0, 0)),
        ],
        out_specs=(
            pl.BlockSpec((step, keys, LANES), lambda i: ((i + half) % (2 * half), 0, 0)),
            pl.BlockSpec((step, SUBLANES, LANES), lambda i: ((i + half) % (2 * half), 0, 0)),
        ),
        scratch_shapes=[pltpu.VMEM((step * body, LANES), f32)],
        compiler_params=pltpu.CompilerParams(vmem_limit_bytes=16 * 2**20),
        cost_estimate=pl.CostEstimate(
            flops=2 * LANES * width * candidates * keys,
            bytes_accessed=candidate_states.size,
            transcendentals=0,
        ),
        name="value",
    )(
        candidate_states.reshape(peers, body, 2 * width),
        channel_readout.reshape(heads, HEAD_SIZE),
    )

    length_lanes = jnp.broadcast_to(candidate_length[:, :, None], (targets, slots, LANES))
    flat = candidate_row.reshape(candidates)
    pair = jnp.arange(candidates, dtype=jnp.int32)
    start = pair // slots * (slots * PACKED) + pair % slots
    start = jnp.sum(jnp.where(flat[None, :] == pair[:, None], start[None, :], 0), axis=1)
    held = place_of(flat // rows, peers, OUT_FLIP) * body + flat % rows * keys
    at = jnp.stack([held, start])
    direct, place = pl.pallas_call(
        direct_kernel,
        out_shape=(
            jax.ShapeDtypeStruct((targets, slots, slots * keys), f32),
            pltpu.SMEM(at.shape, jnp.int32),
        ),
        grid_spec=pltpu.PrefetchScalarGridSpec(
            num_scalar_prefetch=2,
            grid=(targets,),
            in_specs=[
                pl.BlockSpec((1, slots * keys, query_width), lambda t, n, a: (t, 0, 0)),
                pl.BlockSpec((1, tokens, 2 * width), lambda t, n, a: (t, 0, 0)),
                pl.BlockSpec((heads, HEAD_SIZE), lambda t, n, a: (0, 0)),
                pl.BlockSpec((1, slots, LANES), lambda t, n, a: (t, 0, 0)),
            ],
            out_specs=(
                pl.BlockSpec((1, slots, slots * keys), lambda t, n, a: (t, 0, 0)),
                pl.BlockSpec(memory_space=pltpu.SMEM),
            ),
        ),
        compiler_params=pltpu.CompilerParams(vmem_limit_bytes=32 * 2**20),
        cost_estimate=pl.CostEstimate(
            flops=4 * candidate_queries.size * tokens,
            bytes_accessed=2 * candidate_queries.size,
            transcendentals=0,
        ),
        name="direct",
    )(
        target_length,
        at,
        candidate_queries.reshape(targets, slots * keys, query_width),
        target_states,
        direct_readout.reshape(heads, HEAD_SIZE),
        length_lanes,
    )

    queries = target_queries.reshape(targets, tokens, KEY_VALUE_HEADS, share, HEAD_SIZE)
    queries = queries.transpose(0, 2, 4, 1, 3).reshape(
        targets, KEY_VALUE_HEADS, HEAD_SIZE, columns
    )
    token = jnp.arange(columns, dtype=jnp.int32)[None, :] // share
    count = target_length[:, None]
    weight = jnp.where(token < count, 1.0 / count.astype(f32), 0.0)
    direct, factor, first = lax.optimization_barrier((direct, factor, first))
    outgoing = pl.pallas_call(
        functools.partial(channel_kernel, rows),
        out_shape=jax.ShapeDtypeStruct((peers, keys, LANES), f32),
        in_specs=[smem] + [vmem] * 5,
        out_specs=vmem,
        scratch_shapes=[
            pltpu.VMEM((targets, KEY_VALUE_HEADS, slots * keys, HEAD_SIZE), f32),
            pltpu.VMEM((targets * slots * PACKED, LANES), f32),
        ],
        compiler_params=pltpu.CompilerParams(vmem_limit_bytes=32 * 2**20),
        name="channel",
    )(
        place,
        arrived.reshape(peers * body, width),
        queries,
        direct,
        length_lanes,
        weight,
    )
    returned = exchange(outgoing, axis_index_groups=[back_order])
    result = pl.pallas_call(
        functools.partial(finish_kernel, rows),
        out_shape=jax.ShapeDtypeStruct((1, candidates), f32),
        in_specs=[vmem] * 3,
        out_specs=vmem,
        compiler_params=pltpu.CompilerParams(vmem_limit_bytes=16 * 2**20),
        name="finish",
    )(returned, factor, first)
    return result.reshape(candidates)


def solution(mesh):
    in_specs = (
        P(("group", "dp"), None, None, None),
        P(("group", "dp"), None, None),
        P(("group", "dp"), None, None),
        P(("group", "dp"), None, None),
        P(("group", "dp")),
        P(("group", "dp"), None),
        P(("group", "dp"), None),
        P(),
        P(),
    )
    out_specs = P(("group", "dp"))
    return jax.shard_map(
        functools.partial(on_device, peers=mesh.shape["dp"]),
        mesh=mesh,
        in_specs=in_specs,
        out_specs=out_specs,
        check_vma=False,
    )
```

```python
import functools
import math

import jax
import jax.numpy as jnp
from jax import lax
from jax.experimental import pallas as pl
from jax.experimental.pallas import tpu as pltpu
from jax.sharding import PartitionSpec as P

KEY_VALUE_HEADS = 4
HEAD_SIZE = 128
LANES = 128
SUBLANES = 8
MASKED = -1e30
PACKED = 4
KEY_PARTS = 4
OUT_FLIP = 3
BACK_FLIP = 3

bf16 = jnp.bfloat16
f32 = jnp.float32


def turned(i, count, flip):
    return ((i + count // 2) % count) ^ flip


def place_of(device, count, flip):
    return ((device ^ flip) + count // 2) % count


def mirrored(i, count):
    quarter = count // 4
    return (2 - i // quarter) % 4 * quarter + i % quarter


def dot_nt(a, b):
    return lax.dot_general(a, b, (((1,), (1,)), ((), ())), preferred_element_type=f32)


def dot_nn(a, b):
    return lax.dot_general(a, b, (((1,), (0,)), ((), ())), preferred_element_type=f32)


def iota(shape, axis):
    return lax.broadcasted_iota(jnp.int32, shape, axis)


def keys_kernel(states_ref, out_ref, held_ref, sems):
    peers, _, width = out_ref.shape
    parts = KEY_PARTS
    step = peers // parts
    loads, sends = [], []
    for i in range(parts):
        at = pl.ds(i * step, step)
        loads.append(
            pltpu.make_async_copy(states_ref.at[at, :, :width], held_ref.at[at], sems.at[0, i])
        )
        loads[i].start()
    for i in range(parts):
        loads[i].wait()
        size = step if OUT_FLIP == 0 else 1
        for j in range(i * step, (i + 1) * step, size):
            to = pl.ds(mirrored(j ^ OUT_FLIP, peers), size)
            sends.append(
                pltpu.make_async_copy(held_ref.at[j : j + size], out_ref.at[to], sems.at[1, j // size])
            )
            sends[-1].start()
    for copy in sends:
        copy.wait()


def value_kernel(rows, keys, values_ref, readout_ref, factor_ref, first_ref, read_ref):
    peers, body, width = values_ref.shape
    share = readout_ref.shape[0] // KEY_VALUE_HEADS
    wide = LANES // KEY_VALUE_HEADS
    blocks = []
    for g in range(KEY_VALUE_HEADS):
        block = jnp.concatenate(
            [readout_ref[g * share : (g + 1) * share, :].astype(f32)] * (wide // share), axis=0
        )
        none = jnp.zeros_like(block)
        blocks.append(
            jnp.concatenate([block if i == g else none for i in range(KEY_VALUE_HEADS)], axis=1)
        )
    spread = jnp.concatenate(blocks, axis=0).astype(bf16)
    read_ref[...] = dot_nt(values_ref[...].reshape(peers * body, width), spread)
    part = iota((PACKED, LANES), 1) % wide // share
    first_key = (iota((PACKED, LANES), 0) == 0) & (part == 0)
    if rows < PACKED:
        factor_ref[...] = jnp.zeros_like(factor_ref)
    first_ref[...] = jnp.zeros_like(first_ref)
    for p in range(peers):
        to = p ^ BACK_FLIP
        for r in range(rows):
            start = p * body + r * keys
            value = read_ref[pl.ds(start, PACKED, stride=PACKED), :]
            for i in range(1, PACKED):
                value = jnp.where(part == i, read_ref[pl.ds(start + i, PACKED, stride=PACKED), :], value)
            first = read_ref[start : start + 1, :]
            factor_ref[to, pl.ds(r, PACKED, stride=PACKED), :] = jnp.where(first_key, 1.0, value - first)
            first_ref[to, r : r + 1, :] = jnp.where(part[:1] == 0, first, 0.0)


def direct_kernel(
    target_length, at_ref, queries_ref, states_ref, readout_ref, length_ref, out_ref, place_ref
):
    t = pl.program_id(0)

    @pl.when(t == 0)
    def _():
        for i in range(at_ref.shape[0]):
            for j in range(at_ref.shape[1]):
                place_ref[i, j] = at_ref[i, j]

    keys = states_ref.shape[1]
    width = states_ref.shape[2] // 2
    tokens = queries_ref.shape[1]
    slots = length_ref.shape[1]
    heads = readout_ref.shape[0]
    share = heads // KEY_VALUE_HEADS
    scale = math.log2(math.e) / math.sqrt(HEAD_SIZE)
    usable = iota((keys, share * tokens), 0) < target_length[t]
    total = jnp.zeros((1, tokens), f32)
    for g in range(KEY_VALUE_HEADS):
        k = states_ref[0, :, g * HEAD_SIZE : (g + 1) * HEAD_SIZE]
        v = states_ref[0, :, width + g * HEAD_SIZE : width + (g + 1) * HEAD_SIZE]
        q = jnp.concatenate(
            [
                queries_ref[0, :, h * HEAD_SIZE : (h + 1) * HEAD_SIZE]
                for h in range(g * share, (g + 1) * share)
            ],
            axis=0,
        )
        scores = jnp.where(usable, dot_nt(k, q), MASKED)
        weights = jnp.exp2((scores - jnp.max(scores, axis=0, keepdims=True)) * scale)
        read = dot_nt(v, readout_ref[g * share : (g + 1) * share, :])
        read = jnp.concatenate(
            [jnp.broadcast_to(read[:, h : h + 1], (keys, tokens)) for h in range(share)], axis=1
        )
        ratio = jnp.sum(weights * read, axis=0, keepdims=True) / jnp.sum(
            weights, axis=0, keepdims=True
        )
        for h in range(share):
            total = total + ratio[:, h * tokens : (h + 1) * tokens]
    source = tokens // slots
    lane = iota((slots, tokens), 1)
    length = length_ref[0]
    wanted = (lane // source == iota((slots, tokens), 0)) & (lane % source < length)
    total = jnp.where(wanted, jnp.broadcast_to(total, (slots, tokens)), 0.0)
    total = jnp.sum(total, axis=1, keepdims=True) / length.astype(f32)
    out_ref[0] = jnp.where(lane == 0, total, 0.0)


def halves(a, b, bit, lane):
    upper = lane // bit % 2 == 1
    moved = jnp.where(upper, a, b)
    if 2 * bit == LANES:
        moved = pltpu.roll(moved, bit, 1)
    else:
        moved = jnp.take_along_axis(moved, lane + jnp.where(upper, -bit, bit), axis=1)
    return jnp.where(upper, b, a) + moved


def channel_kernel(
    rows,
    place_ref,
    arrived_ref,
    queries_ref,
    direct_ref,
    length_ref,
    weight_ref,
    out_ref,
    keys_ref,
    pooled_ref,
):
    targets = queries_ref.shape[0]
    columns = queries_ref.shape[3]
    slots = direct_ref.shape[1]
    peers = out_ref.shape[0]
    keys = keys_ref.shape[2] // slots
    wide = LANES // KEY_VALUE_HEADS
    share = wide // PACKED
    scale = math.log2(math.e) / math.sqrt(HEAD_SIZE)
    position = iota((keys, slots, columns), 0)
    lane = iota((slots, LANES), 1)
    for t in range(targets):
        for s in range(slots):
            start = pl.multiple_of(place_ref[0, t * slots + s], keys)
            key = arrived_ref[pl.ds(start, keys), :].astype(f32)
            for g in range(KEY_VALUE_HEADS):
                keys_ref[t, g, pl.ds(s, keys, stride=slots), :] = key[
                    :, g * HEAD_SIZE : (g + 1) * HEAD_SIZE
                ]
        usable = position < jnp.concatenate([length_ref[t]] * (columns // LANES), axis=1)[None]
        parts = []
        for g in range(KEY_VALUE_HEADS):
            scores = dot_nn(keys_ref[t, g].astype(bf16), queries_ref[t, g])
            scores = jnp.where(usable, scores.reshape(keys, slots, columns), MASKED)
            weights = jnp.exp2((scores - jnp.max(scores, axis=0, keepdims=True)) * scale)
            weights = weights * (weight_ref[t : t + 1, :] / jnp.sum(weights, axis=0))[None]
            part = weights[:, :, :LANES]
            for i in range(1, columns // LANES):
                part = part + weights[:, :, i * LANES : (i + 1) * LANES]
            parts.append(part)
        for i in range(keys // PACKED):
            part = []
            for k in range(i * PACKED, (i + 1) * PACKED):
                low = halves(parts[0][k], parts[2][k], 2 * wide, lane)
                high = halves(parts[1][k], parts[3][k], 2 * wide, lane)
                part.append(halves(low, high, wide, lane))
            low = halves(part[0], part[2], 2 * share, lane)
            high = halves(part[1], part[3], 2 * share, lane)
            part = halves(low, high, share, lane)
            if i == 0:
                part = jnp.where(lane % wide < share, direct_ref[t], part)
            start = (t * (keys // PACKED) + i) * slots
            pooled_ref[start : start + slots, :] = part
    if rows < PACKED:
        out_ref[...] = jnp.zeros_like(out_ref)
    for i in range(peers):
        p = turned(i, peers, BACK_FLIP)
        for r in range(rows):
            out_ref[i, pl.ds(r, PACKED, stride=PACKED), :] = pooled_ref[
                pl.ds(place_ref[1, p * rows + r], PACKED, stride=slots), :
            ]


def finish_kernel(rows, returned_ref, factor_ref, first_ref, out_ref):
    total = returned_ref[...] * factor_ref[...]
    total = total[:, :SUBLANES] + total[:, SUBLANES:] + first_ref[...]
    total = jnp.sum(total, axis=2, keepdims=True)
    shape = (total.shape[0], SUBLANES, LANES)
    at = turned(iota(shape, 0), shape[0], BACK_FLIP) * rows + iota(shape, 1) % PACKED
    total = jnp.where((iota(shape, 2) == at) & (iota(shape, 1) % PACKED < rows), total, 0.0)
    total = jnp.sum(jnp.sum(total, axis=0), axis=0, keepdims=True)
    out_ref[...] = total[:, : out_ref.shape[1]]


def on_device(
    candidate_queries,
    target_states,
    target_queries,
    candidate_states,
    target_length,
    candidate_length,
    candidate_row,
    direct_readout,
    channel_readout,
    *,
    peers,
):
    targets, slots, keys, query_width = candidate_queries.shape
    tokens = target_queries.shape[1]
    candidates = candidate_states.shape[0]
    width = candidate_states.shape[2] // 2
    heads = query_width // HEAD_SIZE
    share = heads // KEY_VALUE_HEADS
    rows = candidates // peers
    columns = share * tokens
    assert slots == SUBLANES and keys == 2 * SUBLANES and slots * keys == LANES
    assert 4 * heads == LANES and width == 4 * LANES and rows <= 4 and candidates <= LANES

    body = rows * keys
    vmem = pl.BlockSpec(memory_space=pltpu.VMEM)
    smem = pl.BlockSpec(memory_space=pltpu.SMEM)
    assert keys == PACKED * PACKED and rows <= PACKED and share == LANES // KEY_VALUE_HEADS // PACKED
    hbm = pl.BlockSpec(memory_space=pltpu.HBM)
    sent = pl.pallas_call(
        keys_kernel,
        out_shape=jax.ShapeDtypeStruct((peers, body, width), bf16),
        in_specs=[hbm],
        out_specs=hbm,
        scratch_shapes=[
            pltpu.VMEM((peers, body, width), bf16),
            pltpu.SemaphoreType.DMA((2, KEY_PARTS if OUT_FLIP == 0 else peers)),
        ],
        compiler_params=pltpu.CompilerParams(vmem_limit_bytes=16 * 2**20),
        name="keys",
    )(pltpu.with_memory_space_constraint(candidate_states.reshape(peers, body, 2 * width), pltpu.HBM))
    assert peers % 16 == 0
    out_order = [mirrored(i, peers) ^ OUT_FLIP for i in range(peers)]
    back_order = [turned(i, peers, BACK_FLIP) for i in range(peers)]
    exchange = functools.partial(lax.all_to_all, axis_name="dp", split_axis=0, concat_axis=0, tiled=True)
    arrived = exchange(sent, axis_index_groups=[out_order])

    step = peers // 4
    half = 2
    factor, first = pl.pallas_call(
        functools.partial(value_kernel, rows, keys),
        out_shape=(
            jax.ShapeDtypeStruct((peers, keys, LANES), f32),
            jax.ShapeDtypeStruct((peers, SUBLANES, LANES), f32),
        ),
        grid=(peers // step,),
        in_specs=[
            pl.BlockSpec((step, body, width), lambda i: (i, 0, 1)),
            pl.BlockSpec((heads, HEAD_SIZE), lambda i: (0, 0)),
        ],
        out_specs=(
            pl.BlockSpec((step, keys, LANES), lambda i: ((i + half) % (2 * half), 0, 0)),
            pl.BlockSpec((step, SUBLANES, LANES), lambda i: ((i + half) % (2 * half), 0, 0)),
        ),
        scratch_shapes=[pltpu.VMEM((step * body, LANES), f32)],
        compiler_params=pltpu.CompilerParams(vmem_limit_bytes=16 * 2**20),
        cost_estimate=pl.CostEstimate(
            flops=2 * LANES * width * candidates * keys,
            bytes_accessed=candidate_states.size,
            transcendentals=0,
        ),
        name="value",
    )(
        candidate_states.reshape(peers, body, 2 * width),
        channel_readout.reshape(heads, HEAD_SIZE),
    )

    length_lanes = jnp.broadcast_to(candidate_length[:, :, None], (targets, slots, LANES))
    flat = candidate_row.reshape(candidates)
    pair = jnp.arange(candidates, dtype=jnp.int32)
    start = pair // slots * (slots * PACKED) + pair % slots
    start = jnp.sum(jnp.where(flat[None, :] == pair[:, None], start[None, :], 0), axis=1)
    held = mirrored(flat // rows ^ OUT_FLIP, peers) * body + flat % rows * keys
    at = jnp.stack([held, start])
    direct, place = pl.pallas_call(
        direct_kernel,
        out_shape=(
            jax.ShapeDtypeStruct((targets, slots, slots * keys), f32),
            pltpu.SMEM(at.shape, jnp.int32),
        ),
        grid_spec=pltpu.PrefetchScalarGridSpec(
            num_scalar_prefetch=2,
            grid=(targets,),
            in_specs=[
                pl.BlockSpec((1, slots * keys, query_width), lambda t, n, a: (t, 0, 0)),
                pl.BlockSpec((1, tokens, 2 * width), lambda t, n, a: (t, 0, 0)),
                pl.BlockSpec((heads, HEAD_SIZE), lambda t, n, a: (0, 0)),
                pl.BlockSpec((1, slots, LANES), lambda t, n, a: (t, 0, 0)),
            ],
            out_specs=(
                pl.BlockSpec((1, slots, slots * keys), lambda t, n, a: (t, 0, 0)),
                pl.BlockSpec(memory_space=pltpu.SMEM),
            ),
        ),
        compiler_params=pltpu.CompilerParams(vmem_limit_bytes=32 * 2**20),
        cost_estimate=pl.CostEstimate(
            flops=4 * candidate_queries.size * tokens,
            bytes_accessed=2 * candidate_queries.size,
            transcendentals=0,
        ),
        name="direct",
    )(
        target_length,
        at,
        candidate_queries.reshape(targets, slots * keys, query_width),
        target_states,
        direct_readout.reshape(heads, HEAD_SIZE),
        length_lanes,
    )

    queries = target_queries.reshape(targets, tokens, KEY_VALUE_HEADS, share, HEAD_SIZE)
    queries = queries.transpose(0, 2, 4, 1, 3).reshape(
        targets, KEY_VALUE_HEADS, HEAD_SIZE, columns
    )
    token = jnp.arange(columns, dtype=jnp.int32)[None, :] // share
    count = target_length[:, None]
    weight = jnp.where(token < count, 1.0 / count.astype(f32), 0.0)
    direct, factor, first = lax.optimization_barrier((direct, factor, first))
    outgoing = pl.pallas_call(
        functools.partial(channel_kernel, rows),
        out_shape=jax.ShapeDtypeStruct((peers, keys, LANES), f32),
        in_specs=[smem] + [vmem] * 5,
        out_specs=vmem,
        scratch_shapes=[
            pltpu.VMEM((targets, KEY_VALUE_HEADS, slots * keys, HEAD_SIZE), f32),
            pltpu.VMEM((targets * slots * PACKED, LANES), f32),
        ],
        compiler_params=pltpu.CompilerParams(vmem_limit_bytes=32 * 2**20),
        name="channel",
    )(
        place,
        arrived.reshape(peers * body, width),
        queries,
        direct,
        length_lanes,
        weight,
    )
    returned = exchange(outgoing, axis_index_groups=[back_order])
    result = pl.pallas_call(
        functools.partial(finish_kernel, rows),
        out_shape=jax.ShapeDtypeStruct((1, candidates), f32),
        in_specs=[vmem] * 3,
        out_specs=vmem,
        compiler_params=pltpu.CompilerParams(vmem_limit_bytes=16 * 2**20),
        name="finish",
    )(returned, factor, first)
    return result.reshape(candidates)


def solution(mesh):
    in_specs = (
        P(("group", "dp"), None, None, None),
        P(("group", "dp"), None, None),
        P(("group", "dp"), None, None),
        P(("group", "dp"), None, None),
        P(("group", "dp")),
        P(("group", "dp"), None),
        P(("group", "dp"), None),
        P(),
        P(),
    )
    out_specs = P(("group", "dp"))
    return jax.shard_map(
        functools.partial(on_device, peers=mesh.shape["dp"]),
        mesh=mesh,
        in_specs=in_specs,
        out_specs=out_specs,
        check_vma=False,
    )
```

```python
import functools
import math

import jax
import jax.numpy as jnp
from jax import lax
from jax.experimental import pallas as pl
from jax.experimental.pallas import tpu as pltpu
from jax.sharding import PartitionSpec as P

KEY_VALUE_HEADS = 4
HEAD_SIZE = 128
LANES = 128
SUBLANES = 8
MASKED = -1e30
PACKED = 4
KEY_PARTS = 4
OUT_FLIP = 3
BACK_FLIP = 3

bf16 = jnp.bfloat16
f32 = jnp.float32


def turned(i, count):
    quarter = count // 4
    which = i // quarter
    which = 2 * (which == 0) + 1 * (which == 1) + 3 * (which == 2)
    return (which * quarter + i % quarter) ^ BACK_FLIP


def mirrored(i, count):
    quarter = count // 4
    return (2 - i // quarter) % 4 * quarter + i % quarter


def dot_nt(a, b):
    return lax.dot_general(a, b, (((1,), (1,)), ((), ())), preferred_element_type=f32)


def dot_nn(a, b):
    return lax.dot_general(a, b, (((1,), (0,)), ((), ())), preferred_element_type=f32)


def iota(shape, axis):
    return lax.broadcasted_iota(jnp.int32, shape, axis)


def keys_kernel(states_ref, out_ref, held_ref, sems):
    peers, _, width = out_ref.shape
    parts = KEY_PARTS
    step = peers // parts
    loads, sends = [], []
    for i in range(parts):
        at = pl.ds(i * step, step)
        loads.append(
            pltpu.make_async_copy(states_ref.at[at, :, :width], held_ref.at[at], sems.at[0, i])
        )
        loads[i].start()
    for i in range(parts):
        loads[i].wait()
        size = step if OUT_FLIP == 0 else 1
        for j in range(i * step, (i + 1) * step, size):
            to = pl.ds(mirrored(j ^ OUT_FLIP, peers), size)
            sends.append(
                pltpu.make_async_copy(held_ref.at[j : j + size], out_ref.at[to], sems.at[1, j // size])
            )
            sends[-1].start()
    for copy in sends:
        copy.wait()


def value_kernel(rows, keys, values_ref, readout_ref, factor_ref, first_ref, read_ref):
    peers, body, width = values_ref.shape
    share = readout_ref.shape[0] // KEY_VALUE_HEADS
    wide = LANES // KEY_VALUE_HEADS
    blocks = []
    for g in range(KEY_VALUE_HEADS):
        block = jnp.concatenate(
            [readout_ref[g * share : (g + 1) * share, :].astype(f32)] * (wide // share), axis=0
        )
        none = jnp.zeros_like(block)
        blocks.append(
            jnp.concatenate([block if i == g else none for i in range(KEY_VALUE_HEADS)], axis=1)
        )
    spread = jnp.concatenate(blocks, axis=0).astype(bf16)
    read_ref[...] = dot_nt(values_ref[...].reshape(peers * body, width), spread)
    part = iota((PACKED, LANES), 1) % wide // share
    first_key = (iota((PACKED, LANES), 0) == 0) & (part == 0)
    if rows < PACKED:
        factor_ref[...] = jnp.zeros_like(factor_ref)
    first_ref[...] = jnp.zeros_like(first_ref)
    for p in range(peers):
        to = p ^ BACK_FLIP
        for r in range(rows):
            start = p * body + r * keys
            value = read_ref[pl.ds(start, PACKED, stride=PACKED), :]
            for i in range(1, PACKED):
                value = jnp.where(part == i, read_ref[pl.ds(start + i, PACKED, stride=PACKED), :], value)
            first = read_ref[start : start + 1, :]
            factor_ref[to, pl.ds(r, PACKED, stride=PACKED), :] = jnp.where(first_key, 1.0, value - first)
            first_ref[to, r : r + 1, :] = jnp.where(part[:1] == 0, first, 0.0)


def direct_kernel(
    target_length, at_ref, queries_ref, states_ref, readout_ref, length_ref, out_ref, place_ref
):
    t = pl.program_id(0)

    @pl.when(t == 0)
    def _():
        for i in range(at_ref.shape[0]):
            for j in range(at_ref.shape[1]):
                place_ref[i, j] = at_ref[i, j]

    keys = states_ref.shape[1]
    width = states_ref.shape[2] // 2
    tokens = queries_ref.shape[1]
    slots = length_ref.shape[1]
    heads = readout_ref.shape[0]
    share = heads // KEY_VALUE_HEADS
    scale = math.log2(math.e) / math.sqrt(HEAD_SIZE)
    usable = iota((keys, share * tokens), 0) < target_length[t]
    total = jnp.zeros((1, tokens), f32)
    for g in range(KEY_VALUE_HEADS):
        k = states_ref[0, :, g * HEAD_SIZE : (g + 1) * HEAD_SIZE]
        v = states_ref[0, :, width + g * HEAD_SIZE : width + (g + 1) * HEAD_SIZE]
        q = jnp.concatenate(
            [
                queries_ref[0, :, h * HEAD_SIZE : (h + 1) * HEAD_SIZE]
                for h in range(g * share, (g + 1) * share)
            ],
            axis=0,
        )
        scores = jnp.where(usable, dot_nt(k, q), MASKED)
        weights = jnp.exp2((scores - jnp.max(scores, axis=0, keepdims=True)) * scale)
        read = dot_nt(v, readout_ref[g * share : (g + 1) * share, :])
        read = jnp.concatenate(
            [jnp.broadcast_to(read[:, h : h + 1], (keys, tokens)) for h in range(share)], axis=1
        )
        ratio = jnp.sum(weights * read, axis=0, keepdims=True) / jnp.sum(
            weights, axis=0, keepdims=True
        )
        for h in range(share):
            total = total + ratio[:, h * tokens : (h + 1) * tokens]
    source = tokens // slots
    lane = iota((slots, tokens), 1)
    length = length_ref[0]
    wanted = (lane // source == iota((slots, tokens), 0)) & (lane % source < length)
    total = jnp.where(wanted, jnp.broadcast_to(total, (slots, tokens)), 0.0)
    total = jnp.sum(total, axis=1, keepdims=True) / length.astype(f32)
    out_ref[0] = jnp.where(lane == 0, total, 0.0)


def halves(a, b, bit, lane):
    upper = lane // bit % 2 == 1
    moved = jnp.where(upper, a, b)
    if 2 * bit == LANES:
        moved = pltpu.roll(moved, bit, 1)
    else:
        moved = jnp.take_along_axis(moved, lane + jnp.where(upper, -bit, bit), axis=1)
    return jnp.where(upper, b, a) + moved


def channel_kernel(
    rows,
    place_ref,
    arrived_ref,
    queries_ref,
    direct_ref,
    length_ref,
    weight_ref,
    out_ref,
    keys_ref,
    pooled_ref,
):
    targets = queries_ref.shape[0]
    columns = queries_ref.shape[3]
    slots = direct_ref.shape[1]
    peers = out_ref.shape[0]
    keys = keys_ref.shape[2] // slots
    wide = LANES // KEY_VALUE_HEADS
    share = wide // PACKED
    scale = math.log2(math.e) / math.sqrt(HEAD_SIZE)
    position = iota((keys, slots, columns), 0)
    lane = iota((slots, LANES), 1)
    for t in range(targets):
        for s in range(slots):
            start = pl.multiple_of(place_ref[0, t * slots + s], keys)
            key = arrived_ref[pl.ds(start, keys), :].astype(f32)
            for g in range(KEY_VALUE_HEADS):
                keys_ref[t, g, pl.ds(s, keys, stride=slots), :] = key[
                    :, g * HEAD_SIZE : (g + 1) * HEAD_SIZE
                ]
        usable = position < jnp.concatenate([length_ref[t]] * (columns // LANES), axis=1)[None]
        parts = []
        for g in range(KEY_VALUE_HEADS):
            scores = dot_nn(keys_ref[t, g].astype(bf16), queries_ref[t, g])
            scores = jnp.where(usable, scores.reshape(keys, slots, columns), MASKED)
            weights = jnp.exp2((scores - jnp.max(scores, axis=0, keepdims=True)) * scale)
            weights = weights * (weight_ref[t : t + 1, :] / jnp.sum(weights, axis=0))[None]
            part = weights[:, :, :LANES]
            for i in range(1, columns // LANES):
                part = part + weights[:, :, i * LANES : (i + 1) * LANES]
            parts.append(part)
        for i in range(keys // PACKED):
            part = []
            for k in range(i * PACKED, (i + 1) * PACKED):
                low = halves(parts[0][k], parts[2][k], 2 * wide, lane)
                high = halves(parts[1][k], parts[3][k], 2 * wide, lane)
                part.append(halves(low, high, wide, lane))
            low = halves(part[0], part[2], 2 * share, lane)
            high = halves(part[1], part[3], 2 * share, lane)
            part = halves(low, high, share, lane)
            if i == 0:
                part = jnp.where(lane % wide < share, direct_ref[t], part)
            start = (t * (keys // PACKED) + i) * slots
            pooled_ref[start : start + slots, :] = part
    if rows < PACKED:
        out_ref[...] = jnp.zeros_like(out_ref)
    for i in range(peers):
        p = turned(i, peers)
        for r in range(rows):
            out_ref[i, pl.ds(r, PACKED, stride=PACKED), :] = pooled_ref[
                pl.ds(place_ref[1, p * rows + r], PACKED, stride=slots), :
            ]


def finish_kernel(rows, returned_ref, factor_ref, first_ref, out_ref):
    total = returned_ref[...] * factor_ref[...]
    total = total[:, :SUBLANES] + total[:, SUBLANES:] + first_ref[...]
    total = jnp.sum(total, axis=2, keepdims=True)
    shape = (total.shape[0], SUBLANES, LANES)
    at = turned(iota(shape, 0), shape[0]) * rows + iota(shape, 1) % PACKED
    total = jnp.where((iota(shape, 2) == at) & (iota(shape, 1) % PACKED < rows), total, 0.0)
    total = jnp.sum(jnp.sum(total, axis=0), axis=0, keepdims=True)
    out_ref[...] = total[:, : out_ref.shape[1]]


def on_device(
    candidate_queries,
    target_states,
    target_queries,
    candidate_states,
    target_length,
    candidate_length,
    candidate_row,
    direct_readout,
    channel_readout,
    *,
    peers,
):
    targets, slots, keys, query_width = candidate_queries.shape
    tokens = target_queries.shape[1]
    candidates = candidate_states.shape[0]
    width = candidate_states.shape[2] // 2
    heads = query_width // HEAD_SIZE
    share = heads // KEY_VALUE_HEADS
    rows = candidates // peers
    columns = share * tokens
    assert slots == SUBLANES and keys == 2 * SUBLANES and slots * keys == LANES
    assert 4 * heads == LANES and width == 4 * LANES and rows <= 4 and candidates <= LANES

    body = rows * keys
    vmem = pl.BlockSpec(memory_space=pltpu.VMEM)
    smem = pl.BlockSpec(memory_space=pltpu.SMEM)
    assert keys == PACKED * PACKED and rows <= PACKED and share == LANES // KEY_VALUE_HEADS // PACKED
    hbm = pl.BlockSpec(memory_space=pltpu.HBM)
    sent = pl.pallas_call(
        keys_kernel,
        out_shape=jax.ShapeDtypeStruct((peers, body, width), bf16),
        in_specs=[hbm],
        out_specs=hbm,
        scratch_shapes=[
            pltpu.VMEM((peers, body, width), bf16),
            pltpu.SemaphoreType.DMA((2, KEY_PARTS if OUT_FLIP == 0 else peers)),
        ],
        compiler_params=pltpu.CompilerParams(vmem_limit_bytes=16 * 2**20),
        name="keys",
    )(pltpu.with_memory_space_constraint(candidate_states.reshape(peers, body, 2 * width), pltpu.HBM))
    assert peers % 16 == 0
    out_order = [mirrored(i, peers) ^ OUT_FLIP for i in range(peers)]
    back_order = [turned(i, peers) for i in range(peers)]
    exchange = functools.partial(lax.all_to_all, axis_name="dp", split_axis=0, concat_axis=0, tiled=True)
    arrived = exchange(sent, axis_index_groups=[out_order])

    step = peers // 4
    factor, first = pl.pallas_call(
        functools.partial(value_kernel, rows, keys),
        out_shape=(
            jax.ShapeDtypeStruct((peers, keys, LANES), f32),
            jax.ShapeDtypeStruct((peers, SUBLANES, LANES), f32),
        ),
        grid=(peers // step,),
        in_specs=[
            pl.BlockSpec((step, body, width), lambda i: (i, 0, 1)),
            pl.BlockSpec((heads, HEAD_SIZE), lambda i: (0, 0)),
        ],
        out_specs=(
            pl.BlockSpec((step, keys, LANES), lambda i: (3 * (i == 0) + 1 * (i == 1) + 2 * (i == 3), 0, 0)),
            pl.BlockSpec((step, SUBLANES, LANES), lambda i: (3 * (i == 0) + 1 * (i == 1) + 2 * (i == 3), 0, 0)),
        ),
        scratch_shapes=[pltpu.VMEM((step * body, LANES), f32)],
        compiler_params=pltpu.CompilerParams(vmem_limit_bytes=16 * 2**20),
        cost_estimate=pl.CostEstimate(
            flops=2 * LANES * width * candidates * keys,
            bytes_accessed=candidate_states.size,
            transcendentals=0,
        ),
        name="value",
    )(
        candidate_states.reshape(peers, body, 2 * width),
        channel_readout.reshape(heads, HEAD_SIZE),
    )

    length_lanes = jnp.broadcast_to(candidate_length[:, :, None], (targets, slots, LANES))
    flat = candidate_row.reshape(candidates)
    pair = jnp.arange(candidates, dtype=jnp.int32)
    start = pair // slots * (slots * PACKED) + pair % slots
    start = jnp.sum(jnp.where(flat[None, :] == pair[:, None], start[None, :], 0), axis=1)
    held = mirrored(flat // rows ^ OUT_FLIP, peers) * body + flat % rows * keys
    at = jnp.stack([held, start])
    direct, place = pl.pallas_call(
        direct_kernel,
        out_shape=(
            jax.ShapeDtypeStruct((targets, slots, slots * keys), f32),
            pltpu.SMEM(at.shape, jnp.int32),
        ),
        grid_spec=pltpu.PrefetchScalarGridSpec(
            num_scalar_prefetch=2,
            grid=(targets,),
            in_specs=[
                pl.BlockSpec((1, slots * keys, query_width), lambda t, n, a: (t, 0, 0)),
                pl.BlockSpec((1, tokens, 2 * width), lambda t, n, a: (t, 0, 0)),
                pl.BlockSpec((heads, HEAD_SIZE), lambda t, n, a: (0, 0)),
                pl.BlockSpec((1, slots, LANES), lambda t, n, a: (t, 0, 0)),
            ],
            out_specs=(
                pl.BlockSpec((1, slots, slots * keys), lambda t, n, a: (t, 0, 0)),
                pl.BlockSpec(memory_space=pltpu.SMEM),
            ),
        ),
        compiler_params=pltpu.CompilerParams(vmem_limit_bytes=32 * 2**20),
        cost_estimate=pl.CostEstimate(
            flops=4 * candidate_queries.size * tokens,
            bytes_accessed=2 * candidate_queries.size,
            transcendentals=0,
        ),
        name="direct",
    )(
        target_length,
        at,
        candidate_queries.reshape(targets, slots * keys, query_width),
        target_states,
        direct_readout.reshape(heads, HEAD_SIZE),
        length_lanes,
    )

    queries = target_queries.reshape(targets, tokens, KEY_VALUE_HEADS, share, HEAD_SIZE)
    queries = queries.transpose(0, 2, 4, 1, 3).reshape(
        targets, KEY_VALUE_HEADS, HEAD_SIZE, columns
    )
    token = jnp.arange(columns, dtype=jnp.int32)[None, :] // share
    count = target_length[:, None]
    weight = jnp.where(token < count, 1.0 / count.astype(f32), 0.0)
    direct, factor, first = lax.optimization_barrier((direct, factor, first))
    outgoing = pl.pallas_call(
        functools.partial(channel_kernel, rows),
        out_shape=jax.ShapeDtypeStruct((peers, keys, LANES), f32),
        in_specs=[smem] + [vmem] * 5,
        out_specs=vmem,
        scratch_shapes=[
            pltpu.VMEM((targets, KEY_VALUE_HEADS, slots * keys, HEAD_SIZE), f32),
            pltpu.VMEM((targets * slots * PACKED, LANES), f32),
        ],
        compiler_params=pltpu.CompilerParams(vmem_limit_bytes=32 * 2**20),
        name="channel",
    )(
        place,
        arrived.reshape(peers * body, width),
        queries,
        direct,
        length_lanes,
        weight,
    )
    returned = exchange(outgoing, axis_index_groups=[back_order])
    result = pl.pallas_call(
        functools.partial(finish_kernel, rows),
        out_shape=jax.ShapeDtypeStruct((1, candidates), f32),
        in_specs=[vmem] * 3,
        out_specs=vmem,
        compiler_params=pltpu.CompilerParams(vmem_limit_bytes=16 * 2**20),
        name="finish",
    )(returned, factor, first)
    return result.reshape(candidates)


def solution(mesh):
    in_specs = (
        P(("group", "dp"), None, None, None),
        P(("group", "dp"), None, None),
        P(("group", "dp"), None, None),
        P(("group", "dp"), None, None),
        P(("group", "dp")),
        P(("group", "dp"), None),
        P(("group", "dp"), None),
        P(),
        P(),
    )
    out_specs = P(("group", "dp"))
    return jax.shard_map(
        functools.partial(on_device, peers=mesh.shape["dp"]),
        mesh=mesh,
        in_specs=in_specs,
        out_specs=out_specs,
        check_vma=False,
    )
```

```python
import functools
import math

import jax
import jax.numpy as jnp
from jax import lax
from jax.experimental import pallas as pl
from jax.experimental.pallas import tpu as pltpu
from jax.sharding import PartitionSpec as P

KEY_VALUE_HEADS = 4
HEAD_SIZE = 128
LANES = 128
SUBLANES = 8
MASKED = -1e30
PACKED = 4
KEY_PARTS = 4
OUT_FLIP = 0
BACK_FLIP = 3

bf16 = jnp.bfloat16
f32 = jnp.float32


def turned(i, count, flip):
    return ((i + count // 2) % count) ^ flip


def place_of(device, count, flip):
    return ((device ^ flip) + count // 2) % count


def mirrored(i, count):
    quarter = count // 4
    return (2 - i // quarter) % 4 * quarter + i % quarter


def dot_nt(a, b):
    return lax.dot_general(a, b, (((1,), (1,)), ((), ())), preferred_element_type=f32)


def dot_nn(a, b):
    return lax.dot_general(a, b, (((1,), (0,)), ((), ())), preferred_element_type=f32)


def iota(shape, axis):
    return lax.broadcasted_iota(jnp.int32, shape, axis)


def keys_kernel(states_ref, out_ref, held_ref, sems):
    peers, _, width = out_ref.shape
    parts = KEY_PARTS
    step = peers // parts
    loads, sends = [], []
    for i in range(parts):
        at = pl.ds(i * step, step)
        loads.append(
            pltpu.make_async_copy(states_ref.at[at, :, :width], held_ref.at[at], sems.at[0, i])
        )
        loads[i].start()
    for i in range(parts):
        loads[i].wait()
        size = step if OUT_FLIP == 0 else 1
        for j in range(i * step, (i + 1) * step, size):
            to = pl.ds(mirrored(j ^ OUT_FLIP, peers), size)
            sends.append(
                pltpu.make_async_copy(held_ref.at[j : j + size], out_ref.at[to], sems.at[1, j // size])
            )
            sends[-1].start()
    for copy in sends:
        copy.wait()


def value_kernel(rows, keys, values_ref, readout_ref, factor_ref, first_ref, read_ref):
    peers, body, width = values_ref.shape
    share = readout_ref.shape[0] // KEY_VALUE_HEADS
    wide = LANES // KEY_VALUE_HEADS
    blocks = []
    for g in range(KEY_VALUE_HEADS):
        block = jnp.concatenate(
            [readout_ref[g * share : (g + 1) * share, :].astype(f32)] * (wide // share), axis=0
        )
        none = jnp.zeros_like(block)
        blocks.append(
            jnp.concatenate([block if i == g else none for i in range(KEY_VALUE_HEADS)], axis=1)
        )
    spread = jnp.concatenate(blocks, axis=0).astype(bf16)
    read_ref[...] = dot_nt(values_ref[...].reshape(peers * body, width), spread)
    part = iota((PACKED, LANES), 1) % wide // share
    first_key = (iota((PACKED, LANES), 0) == 0) & (part == 0)
    if rows < PACKED:
        factor_ref[...] = jnp.zeros_like(factor_ref)
    first_ref[...] = jnp.zeros_like(first_ref)
    for p in range(peers):
        to = p ^ BACK_FLIP
        for r in range(rows):
            start = p * body + r * keys
            value = read_ref[pl.ds(start, PACKED, stride=PACKED), :]
            for i in range(1, PACKED):
                value = jnp.where(part == i, read_ref[pl.ds(start + i, PACKED, stride=PACKED), :], value)
            first = read_ref[start : start + 1, :]
            factor_ref[to, pl.ds(r, PACKED, stride=PACKED), :] = jnp.where(first_key, 1.0, value - first)
            first_ref[to, r : r + 1, :] = jnp.where(part[:1] == 0, first, 0.0)


def direct_kernel(
    target_length, at_ref, queries_ref, states_ref, readout_ref, length_ref, out_ref, place_ref
):
    t = pl.program_id(0)

    @pl.when(t == 0)
    def _():
        for i in range(at_ref.shape[0]):
            for j in range(at_ref.shape[1]):
                place_ref[i, j] = at_ref[i, j]

    keys = states_ref.shape[1]
    width = states_ref.shape[2] // 2
    tokens = queries_ref.shape[1]
    slots = length_ref.shape[1]
    heads = readout_ref.shape[0]
    share = heads // KEY_VALUE_HEADS
    scale = math.log2(math.e) / math.sqrt(HEAD_SIZE)
    usable = iota((keys, share * tokens), 0) < target_length[t]
    total = jnp.zeros((1, tokens), f32)
    for g in range(KEY_VALUE_HEADS):
        k = states_ref[0, :, g * HEAD_SIZE : (g + 1) * HEAD_SIZE]
        v = states_ref[0, :, width + g * HEAD_SIZE : width + (g + 1) * HEAD_SIZE]
        q = jnp.concatenate(
            [
                queries_ref[0, :, h * HEAD_SIZE : (h + 1) * HEAD_SIZE]
                for h in range(g * share, (g + 1) * share)
            ],
            axis=0,
        )
        scores = jnp.where(usable, dot_nt(k, q), MASKED)
        weights = jnp.exp2((scores - jnp.max(scores, axis=0, keepdims=True)) * scale)
        read = dot_nt(v, readout_ref[g * share : (g + 1) * share, :])
        read = jnp.concatenate(
            [jnp.broadcast_to(read[:, h : h + 1], (keys, tokens)) for h in range(share)], axis=1
        )
        ratio = jnp.sum(weights * read, axis=0, keepdims=True) / jnp.sum(
            weights, axis=0, keepdims=True
        )
        for h in range(share):
            total = total + ratio[:, h * tokens : (h + 1) * tokens]
    source = tokens // slots
    lane = iota((slots, tokens), 1)
    length = length_ref[0]
    wanted = (lane // source == iota((slots, tokens), 0)) & (lane % source < length)
    total = jnp.where(wanted, jnp.broadcast_to(total, (slots, tokens)), 0.0)
    total = jnp.sum(total, axis=1, keepdims=True) / length.astype(f32)
    out_ref[0] = jnp.where(lane == 0, total, 0.0)


def halves(a, b, bit, lane):
    upper = lane // bit % 2 == 1
    moved = jnp.where(upper, a, b)
    if 2 * bit == LANES:
        moved = pltpu.roll(moved, bit, 1)
    else:
        moved = jnp.take_along_axis(moved, lane + jnp.where(upper, -bit, bit), axis=1)
    return jnp.where(upper, b, a) + moved


def channel_kernel(
    rows,
    place_ref,
    arrived_ref,
    queries_ref,
    direct_ref,
    length_ref,
    weight_ref,
    out_ref,
    keys_ref,
    pooled_ref,
):
    targets = queries_ref.shape[0]
    columns = queries_ref.shape[3]
    slots = direct_ref.shape[1]
    peers = out_ref.shape[0]
    keys = keys_ref.shape[2] // slots
    wide = LANES // KEY_VALUE_HEADS
    share = wide // PACKED
    scale = math.log2(math.e) / math.sqrt(HEAD_SIZE)
    position = iota((keys, slots, columns), 0)
    lane = iota((slots, LANES), 1)
    for t in range(targets):
        for s in range(slots):
            start = pl.multiple_of(place_ref[0, t * slots + s], keys)
            key = arrived_ref[pl.ds(start, keys), :].astype(f32)
            for g in range(KEY_VALUE_HEADS):
                keys_ref[t, g, pl.ds(s, keys, stride=slots), :] = key[
                    :, g * HEAD_SIZE : (g + 1) * HEAD_SIZE
                ]
        usable = position < jnp.concatenate([length_ref[t]] * (columns // LANES), axis=1)[None]
        parts = []
        for g in range(KEY_VALUE_HEADS):
            scores = dot_nn(keys_ref[t, g].astype(bf16), queries_ref[t, g])
            scores = jnp.where(usable, scores.reshape(keys, slots, columns), MASKED)
            weights = jnp.exp2((scores - jnp.max(scores, axis=0, keepdims=True)) * scale)
            weights = weights * (weight_ref[t : t + 1, :] / jnp.sum(weights, axis=0))[None]
            part = weights[:, :, :LANES]
            for i in range(1, columns // LANES):
                part = part + weights[:, :, i * LANES : (i + 1) * LANES]
            parts.append(part)
        for i in range(keys // PACKED):
            part = []
            for k in range(i * PACKED, (i + 1) * PACKED):
                low = halves(parts[0][k], parts[2][k], 2 * wide, lane)
                high = halves(parts[1][k], parts[3][k], 2 * wide, lane)
                part.append(halves(low, high, wide, lane))
            low = halves(part[0], part[2], 2 * share, lane)
            high = halves(part[1], part[3], 2 * share, lane)
            part = halves(low, high, share, lane)
            if i == 0:
                part = jnp.where(lane % wide < share, direct_ref[t], part)
            start = (t * (keys // PACKED) + i) * slots
            pooled_ref[start : start + slots, :] = part
    if rows < PACKED:
        out_ref[...] = jnp.zeros_like(out_ref)
    for i in range(peers):
        p = turned(i, peers, BACK_FLIP)
        for r in range(rows):
            out_ref[i, pl.ds(r, PACKED, stride=PACKED), :] = pooled_ref[
                pl.ds(place_ref[1, p * rows + r], PACKED, stride=slots), :
            ]


def finish_kernel(rows, returned_ref, factor_ref, first_ref, out_ref):
    total = returned_ref[...] * factor_ref[...]
    total = total[:, :SUBLANES] + total[:, SUBLANES:] + first_ref[...]
    total = jnp.sum(total, axis=2, keepdims=True)
    shape = (total.shape[0], SUBLANES, LANES)
    at = turned(iota(shape, 0), shape[0], BACK_FLIP) * rows + iota(shape, 1) % PACKED
    total = jnp.where((iota(shape, 2) == at) & (iota(shape, 1) % PACKED < rows), total, 0.0)
    total = jnp.sum(jnp.sum(total, axis=0), axis=0, keepdims=True)
    out_ref[...] = total[:, : out_ref.shape[1]]


def on_device(
    candidate_queries,
    target_states,
    target_queries,
    candidate_states,
    target_length,
    candidate_length,
    candidate_row,
    direct_readout,
    channel_readout,
    *,
    peers,
):
    targets, slots, keys, query_width = candidate_queries.shape
    tokens = target_queries.shape[1]
    candidates = candidate_states.shape[0]
    width = candidate_states.shape[2] // 2
    heads = query_width // HEAD_SIZE
    share = heads // KEY_VALUE_HEADS
    rows = candidates // peers
    columns = share * tokens
    assert slots == SUBLANES and keys == 2 * SUBLANES and slots * keys == LANES
    assert 4 * heads == LANES and width == 4 * LANES and rows <= 4 and candidates <= LANES

    body = rows * keys
    vmem = pl.BlockSpec(memory_space=pltpu.VMEM)
    smem = pl.BlockSpec(memory_space=pltpu.SMEM)
    assert keys == PACKED * PACKED and rows <= PACKED and share == LANES // KEY_VALUE_HEADS // PACKED
    hbm = pl.BlockSpec(memory_space=pltpu.HBM)
    sent = pl.pallas_call(
        keys_kernel,
        out_shape=jax.ShapeDtypeStruct((peers, body, width), bf16),
        in_specs=[hbm],
        out_specs=hbm,
        scratch_shapes=[
            pltpu.VMEM((peers, body, width), bf16),
            pltpu.SemaphoreType.DMA((2, KEY_PARTS if OUT_FLIP == 0 else peers)),
        ],
        compiler_params=pltpu.CompilerParams(vmem_limit_bytes=16 * 2**20),
        name="keys",
    )(pltpu.with_memory_space_constraint(candidate_states.reshape(peers, body, 2 * width), pltpu.HBM))
    assert peers % 16 == 0
    out_order = [mirrored(i, peers) ^ OUT_FLIP for i in range(peers)]
    back_order = [turned(i, peers, BACK_FLIP) for i in range(peers)]
    exchange = functools.partial(lax.all_to_all, axis_name="dp", split_axis=0, concat_axis=0, tiled=True)
    arrived = exchange(sent, axis_index_groups=[out_order])

    step = peers // 4
    half = 2
    factor, first = pl.pallas_call(
        functools.partial(value_kernel, rows, keys),
        out_shape=(
            jax.ShapeDtypeStruct((peers, keys, LANES), f32),
            jax.ShapeDtypeStruct((peers, SUBLANES, LANES), f32),
        ),
        grid=(peers // step,),
        in_specs=[
            pl.BlockSpec((step, body, width), lambda i: (i, 0, 1)),
            pl.BlockSpec((heads, HEAD_SIZE), lambda i: (0, 0)),
        ],
        out_specs=(
            pl.BlockSpec((step, keys, LANES), lambda i: ((i + half) % (2 * half), 0, 0)),
            pl.BlockSpec((step, SUBLANES, LANES), lambda i: ((i + half) % (2 * half), 0, 0)),
        ),
        scratch_shapes=[pltpu.VMEM((step * body, LANES), f32)],
        compiler_params=pltpu.CompilerParams(vmem_limit_bytes=16 * 2**20),
        cost_estimate=pl.CostEstimate(
            flops=2 * LANES * width * candidates * keys,
            bytes_accessed=candidate_states.size,
            transcendentals=0,
        ),
        name="value",
    )(
        candidate_states.reshape(peers, body, 2 * width),
        channel_readout.reshape(heads, HEAD_SIZE),
    )

    length_lanes = jnp.broadcast_to(candidate_length[:, :, None], (targets, slots, LANES))
    flat = candidate_row.reshape(candidates)
    pair = jnp.arange(candidates, dtype=jnp.int32)
    start = pair // slots * (slots * PACKED) + pair % slots
    start = jnp.sum(jnp.where(flat[None, :] == pair[:, None], start[None, :], 0), axis=1)
    held = mirrored(flat // rows ^ OUT_FLIP, peers) * body + flat % rows * keys
    at = jnp.stack([held, start])
    direct, place = pl.pallas_call(
        direct_kernel,
        out_shape=(
            jax.ShapeDtypeStruct((targets, slots, slots * keys), f32),
            pltpu.SMEM(at.shape, jnp.int32),
        ),
        grid_spec=pltpu.PrefetchScalarGridSpec(
            num_scalar_prefetch=2,
            grid=(targets,),
            in_specs=[
                pl.BlockSpec((1, slots * keys, query_width), lambda t, n, a: (t, 0, 0)),
                pl.BlockSpec((1, tokens, 2 * width), lambda t, n, a: (t, 0, 0)),
                pl.BlockSpec((heads, HEAD_SIZE), lambda t, n, a: (0, 0)),
                pl.BlockSpec((1, slots, LANES), lambda t, n, a: (t, 0, 0)),
            ],
            out_specs=(
                pl.BlockSpec((1, slots, slots * keys), lambda t, n, a: (t, 0, 0)),
                pl.BlockSpec(memory_space=pltpu.SMEM),
            ),
        ),
        compiler_params=pltpu.CompilerParams(vmem_limit_bytes=32 * 2**20),
        cost_estimate=pl.CostEstimate(
            flops=4 * candidate_queries.size * tokens,
            bytes_accessed=2 * candidate_queries.size,
            transcendentals=0,
        ),
        name="direct",
    )(
        target_length,
        at,
        candidate_queries.reshape(targets, slots * keys, query_width),
        target_states,
        direct_readout.reshape(heads, HEAD_SIZE),
        length_lanes,
    )

    queries = target_queries.reshape(targets, tokens, KEY_VALUE_HEADS, share, HEAD_SIZE)
    queries = queries.transpose(0, 2, 4, 1, 3).reshape(
        targets, KEY_VALUE_HEADS, HEAD_SIZE, columns
    )
    token = jnp.arange(columns, dtype=jnp.int32)[None, :] // share
    count = target_length[:, None]
    weight = jnp.where(token < count, 1.0 / count.astype(f32), 0.0)
    direct, factor, first = lax.optimization_barrier((direct, factor, first))
    outgoing = pl.pallas_call(
        functools.partial(channel_kernel, rows),
        out_shape=jax.ShapeDtypeStruct((peers, keys, LANES), f32),
        in_specs=[smem] + [vmem] * 5,
        out_specs=vmem,
        scratch_shapes=[
            pltpu.VMEM((targets, KEY_VALUE_HEADS, slots * keys, HEAD_SIZE), f32),
            pltpu.VMEM((targets * slots * PACKED, LANES), f32),
        ],
        compiler_params=pltpu.CompilerParams(vmem_limit_bytes=32 * 2**20),
        name="channel",
    )(
        place,
        arrived.reshape(peers * body, width),
        queries,
        direct,
        length_lanes,
        weight,
    )
    returned = exchange(outgoing, axis_index_groups=[back_order])
    result = pl.pallas_call(
        functools.partial(finish_kernel, rows),
        out_shape=jax.ShapeDtypeStruct((1, candidates), f32),
        in_specs=[vmem] * 3,
        out_specs=vmem,
        compiler_params=pltpu.CompilerParams(vmem_limit_bytes=16 * 2**20),
        name="finish",
    )(returned, factor, first)
    return result.reshape(candidates)


def solution(mesh):
    in_specs = (
        P(("group", "dp"), None, None, None),
        P(("group", "dp"), None, None),
        P(("group", "dp"), None, None),
        P(("group", "dp"), None, None),
        P(("group", "dp")),
        P(("group", "dp"), None),
        P(("group", "dp"), None),
        P(),
        P(),
    )
    out_specs = P(("group", "dp"))
    return jax.shard_map(
        functools.partial(on_device, peers=mesh.shape["dp"]),
        mesh=mesh,
        in_specs=in_specs,
        out_specs=out_specs,
        check_vma=False,
    )
```
